256 devices in a mesh: dp: 8 (over z_lo, y), seq: 32 (over x, z_hi, core).
Axes of the slice: x: 4, y: 4, z: 8 (z_hi: 4, z_lo: 2; z = z_hi * 2 + z_lo), core: 2. Of those that a mesh axis runs over, the one named last changes fastest.
Arguments:
- query: bfloat16 [8, 4096, 4096], P('dp', 'seq'), may hold values from -6 to 6
- key_stream: bfloat16 [8, 4096, 4096], P('dp', 'seq'), may hold values from -6 to 6
- value_stream: bfloat16 [8, 4096, 4096], P('dp', 'seq'), may hold values from -6 to 6
- upstream: bfloat16 [8, 4096, 4096], P('dp', 'seq'), may hold values from -6 to 6
- bases: int32 [8, 4096], P('dp', 'seq'), may hold values from 0 to 3
- base_rows: bfloat16 [4, 4096], replicated, may hold values from -6 to 6
- long_filter: float32 [4096, 4096], P('seq', 'dp'), may hold values from -6 to 6
- skip_weight: float32 [4096], P('seq'), may hold values from -4 to 4
Outputs:
- query_grad: bfloat16 [8, 4096, 4096], P('dp', 'seq')
- key_grad: bfloat16 [8, 4096, 4096], P('dp', 'seq')
- value_grad: bfloat16 [8, 4096, 4096], P('dp', 'seq')
- filter_grad: float32 [4096, 4096], P('seq', 'dp')
The draws below stay inside these ranges and needn't reach their ends.
Inputs may be any that keep to these rules, and one draw needn't show every extreme that they name: `bases`: each entry names one base.
All inputs are finite; a program needn't handle non-finite values.
Results may differ from the reference program's by a relative error of at most 0.018.
Values may be sent and summed in bfloat16 or wider, within the bound.
No kernel may reach another device: no remote copies, remote signals or barrier semaphores. Data moves between devices by JAX's collectives and lax.ppermute only.
A program may use at most 192 MiB of HBM per device.

```python
import jax
import jax.numpy as jnp
from jax import lax

D = 4096
BASES = 4
L = 4096
SEQS = 8


def set_ends(values, stream_key, least, high):
    longest = values.shape.index(max(values.shape))
    spots = []
    for shift in (0, 1):
        where = [jax.random.randint(jax.random.fold_in(stream_key, axis), (), 0, length) for axis, length in enumerate(values.shape)]
        where[longest] = (where[longest] + shift) % values.shape[longest]
        spots.append(tuple(where))
    return values.at[spots[0]].set(least).at[spots[1]].set(high)


def block_scale(stream_key, dims, cuts, least, top_value):
    def one(position, blocks):
        heights = jax.random.uniform(jax.random.fold_in(jax.random.fold_in(stream_key, 6), position), (blocks,), jnp.float32, least / len(cuts), top_value / len(cuts))
        return jnp.repeat(jnp.exp(heights), dims[position] // blocks).reshape((-1,) + (1,) * (len(dims) - position - 1))

    gain = one(*cuts[0])
    for cut in cuts[1:]:
        gain = gain * one(*cut)
    return gain


def bell_draw(key, dims, width, reach, pieces=(), held_as=jnp.bfloat16):
    gain = block_scale(key, dims, pieces, -0.22, 0.18) if pieces else 1.0
    drawn = jax.random.normal(key, dims, jnp.float32) * width * gain
    return jnp.minimum(jnp.maximum(drawn, -reach), reach).astype(held_as)


def setup_inputs(seed: int = 0) -> dict:
    key_of = jax.random.split(jax.random.key(seed), 9)
    return {
        "query": bell_draw(key_of[0], (SEQS, L, D), 1.0, 6.0, ((0, 8), (1, 32))),
        "key_stream": bell_draw(key_of[1], (SEQS, L, D), 1.0, 6.0, ((0, 8), (1, 32))),
        "value_stream": bell_draw(key_of[2], (SEQS, L, D), 1.0, 6.0, ((0, 8), (1, 32))),
        "upstream": bell_draw(key_of[3], (SEQS, L, D), 1.0, 6.0, ((0, 8), (1, 32))),
        "bases": set_ends(jax.random.randint(key_of[4], (SEQS, L), 0, BASES), jax.random.fold_in(key_of[4], 1), 0, BASES - 1).astype(jnp.int32),
        "base_rows": bell_draw(key_of[5], (BASES, D), 1.0, 6.0),
        "long_filter": bell_draw(key_of[6], (D, L), 1.0, 6.0, ((0, 32), (1, 8)), jnp.float32),
        "skip_weight": bell_draw(key_of[7], (D,), 1.0, 4.0, ((0, 32),), jnp.float32),
    }


def reference(query, key_stream, value_stream, upstream, bases, base_rows, long_filter, skip_weight):
    points = 2 * L
    filter_scale = L ** -0.5
    filter_spec = jnp.fft.rfft(long_filter, n=points, axis=1).T * filter_scale

    def one_sequence(carry, items):
        query_seq, key_seq, value_seq, upstream_seq, bases_seq = items
        gated = (key_seq.astype(jnp.float32) * value_seq.astype(jnp.float32)).astype(jnp.bfloat16)
        out_grad = upstream_seq.astype(jnp.float32) - base_rows[bases_seq].astype(jnp.float32)
        conv_grad = (out_grad * query_seq.astype(jnp.float32)).astype(jnp.bfloat16)
        gated_wide = gated.astype(jnp.float32)
        grad_wide = conv_grad.astype(jnp.float32)
        gated_spec = jnp.fft.rfft(gated_wide, n=points, axis=0)
        grad_spec = jnp.fft.rfft(grad_wide, n=points, axis=0)
        conv_out = jnp.fft.irfft(gated_spec * filter_spec, n=points, axis=0)[:L]
        conv_out = (conv_out + skip_weight * gated_wide).astype(jnp.bfloat16)
        corr_out = jnp.fft.irfft(grad_spec * jnp.conj(filter_spec), n=points, axis=0)[:L]
        corr_out = (corr_out + skip_weight * grad_wide).astype(jnp.bfloat16)
        tap_part = jnp.fft.irfft(jnp.conj(gated_spec) * grad_spec, n=points, axis=0)[:L]
        query_grad = (out_grad * conv_out.astype(jnp.float32)).astype(jnp.bfloat16)
        key_grad = (corr_out.astype(jnp.float32) * value_seq.astype(jnp.float32)).astype(jnp.bfloat16)
        value_grad = (corr_out.astype(jnp.float32) * key_seq.astype(jnp.float32)).astype(jnp.bfloat16)
        return carry + tap_part, (query_grad, key_grad, value_grad)

    start_sum = jnp.zeros((L, D), jnp.float32)
    total, grads = lax.scan(one_sequence, start_sum, (query, key_stream, value_stream, upstream, bases))
    return grads[0], grads[1], grads[2], total.T * filter_scale
```

```python
import math

import jax
import jax.numpy as jnp
import ml_dtypes
import numpy as np
from jax import lax
from jax.experimental import pallas as pl
from jax.experimental.pallas import tpu as pltpu
from jax.sharding import PartitionSpec as P

LANES = 128
SUB = 8
VMEM_BYTES = 56 * 1024 * 1024


def transform_tables(blocks, rows, scale):
    points = 2 * blocks * rows
    half = rows // 2
    low = np.arange(blocks)[:, None, None]
    point = np.arange(blocks)[None, None, :] * rows + np.arange(rows)[None, :, None]
    angle = 2.0 * math.pi / points * (low * point % points)
    first = np.stack([np.cos(angle), -np.sin(angle)], axis=1)
    first[0, 1] = np.where(np.arange(blocks) % 2 == 0, 1.0, -1.0)[None, :]
    first = first.reshape(2 * blocks, rows // SUB, SUB, blocks)
    ahead = np.einsum("mhaj,ab->hmajb", first, np.eye(SUB))
    ahead = ahead.reshape(rows // SUB, 2 * blocks * SUB, blocks * SUB)
    back = np.ascontiguousarray(np.swapaxes(ahead, 1, 2))

    row = np.arange(rows)[None, :]
    high = np.arange(rows)[:, None]
    angle = 2.0 * math.pi / rows * (high * row % rows)
    cosine, sine = np.cos(angle), np.sin(angle)
    usual = np.block([[cosine, sine], [-sine, cosine]])
    odd = 2.0 * math.pi / (2 * rows) * ((2 * high[:half] + 1) * row % (2 * rows))
    blank = np.zeros((half, rows))
    special = np.block(
        [
            [cosine[:half], blank],
            [blank, np.cos(odd)],
            [-sine[:half], blank],
            [blank, -np.sin(odd)],
        ]
    )
    special[rows, :rows] = np.where(np.arange(rows) % 2 == 0, 1.0, -1.0)
    second = np.stack([special, usual])
    weight = np.full((2, 2 * rows, 1), 2.0 / points)
    weight[0, 0] = weight[0, rows] = 1.0 / points
    undo = np.ascontiguousarray(np.swapaxes(second * weight * scale, 1, 2))
    return tuple(table.astype(ml_dtypes.bfloat16) for table in (ahead, back, second, undo))


def dot(left, right):
    return jnp.dot(left, right, preferred_element_type=jnp.float32)


def readout(bases_ref, rows_ref, columns):
    letters = bases_ref[...]
    picked = rows_ref[0:1, columns].astype(jnp.float32)
    for letter in range(1, rows_ref.shape[0]):
        picked = jnp.where(
            letters == letter, rows_ref[letter : letter + 1, columns].astype(jnp.float32), picked
        )
    return picked


def gate_kernel(query_ref, key_ref, value_ref, upstream_ref, bases_ref, rows_ref, out_ref):
    tokens = query_ref.shape[0]
    for block in range(out_ref.shape[0]):
        columns = slice(block * LANES, (block + 1) * LANES)
        gated = key_ref[:, columns].astype(jnp.float32) * value_ref[:, columns].astype(jnp.float32)
        out_grad = upstream_ref[:, columns].astype(jnp.float32) - readout(bases_ref, rows_ref, columns)
        grad = out_grad * query_ref[:, columns].astype(jnp.float32)
        out_ref[block, :tokens, :] = gated.astype(jnp.bfloat16)
        out_ref[block, tokens:, :] = grad.astype(jnp.bfloat16)


def ungate_kernel(back_ref, key_ref, value_ref, upstream_ref, bases_ref, rows_ref, query_out, key_out, value_out):
    tokens = key_ref.shape[0]
    for block in range(back_ref.shape[0]):
        columns = slice(block * LANES, (block + 1) * LANES)
        conv = back_ref[block, :tokens, :].astype(jnp.float32)
        corr = back_ref[block, tokens:, :].astype(jnp.float32)
        out_grad = upstream_ref[:, columns].astype(jnp.float32) - readout(bases_ref, rows_ref, columns)
        query_out[:, columns] = (out_grad * conv).astype(jnp.bfloat16)
        key_out[:, columns] = (corr * value_ref[:, columns].astype(jnp.float32)).astype(jnp.bfloat16)
        value_out[:, columns] = (corr * key_ref[:, columns].astype(jnp.float32)).astype(jnp.bfloat16)


def first_stage(load, ahead_ref, mid_ref):
    for pair in range(ahead_ref.shape[0] // 2):
        both = load(pair)
        for part in range(2):
            step = 2 * pair + part
            piece = both[:, part * SUB : (part + 1) * SUB, :]
            piece = piece.reshape(piece.shape[0] * SUB, piece.shape[2]).astype(jnp.bfloat16)
            mid = dot(ahead_ref[step], piece)
            mid_ref[:, step * SUB : (step + 1) * SUB, :] = mid.reshape(-1, SUB, mid.shape[1])


def last_stage(back_ref, mid_ref, step):
    piece = mid_ref[:, step * SUB : (step + 1) * SUB, :]
    piece = piece.reshape(piece.shape[0] * SUB, piece.shape[2]).astype(jnp.bfloat16)
    out = dot(back_ref[step], piece)
    return out.reshape(-1, SUB, out.shape[1])


def group_of(mid_ref, group):
    both = mid_ref[pl.ds(2 * group, 2)]
    return both.reshape(2 * both.shape[1], both.shape[2])


def taps_kernel(taps_ref, ahead_ref, second_ref, spectrum_ref, mid_ref):
    first_stage(
        lambda pair: taps_ref[:, pair * 2 * SUB : (pair + 1) * 2 * SUB, :].astype(jnp.float32), ahead_ref, mid_ref
    )

    def work(group, which):
        mid = group_of(mid_ref, group).astype(jnp.bfloat16)
        spectrum_ref[group] = dot(second_ref[which], mid)

    work(0, 0)

    @pl.loop(1, spectrum_ref.shape[0])
    def _(group):
        work(group, 1)


def times(left, right, conjugate, first_group):
    half = left.shape[0] // 2
    left_real, left_imag = left[:half], left[half:]
    right_real, right_imag = right[:half], right[half:]
    real_real, imag_imag = left_real * right_real, left_imag * right_imag
    if conjugate:
        real = real_real + imag_imag
        imag = left_imag * right_real - left_real * right_imag
    else:
        real = real_real - imag_imag
        imag = left_imag * right_real + left_real * right_imag
    if first_group:
        apart = lax.broadcasted_iota(jnp.int32, real.shape, 0) == 0
        real = jnp.where(apart, real_real, real)
        imag = jnp.where(apart, imag_imag, imag)
    return jnp.concatenate([real, imag], axis=0)


def main_kernel(
    both_ref, filter_ref, skip_ref, ahead_ref, back_ref, second_ref, undo_ref, out_ref, cross_ref, mid_ref
):
    tokens = both_ref.shape[1] // 2

    def load(pair):
        rows = slice(pair * 2 * SUB, (pair + 1) * 2 * SUB)
        more = slice(tokens + pair * 2 * SUB, tokens + (pair + 1) * 2 * SUB)
        return jnp.concatenate([both_ref[:, rows, :], both_ref[:, more, :]], axis=2).astype(jnp.float32)

    first_stage(load, ahead_ref, mid_ref)

    def work(group, which):
        spectrum = dot(second_ref[which], group_of(mid_ref, group).astype(jnp.bfloat16))
        gated, grad = spectrum[:, :LANES], spectrum[:, LANES:]
        taps = filter_ref[group]
        conv = times(gated, taps, False, which == 0)
        corr = times(grad, taps, True, which == 0)
        cross_ref[group] = times(grad, gated, True, which == 0)
        product = jnp.concatenate([conv, corr], axis=1).astype(jnp.bfloat16)
        undone = dot(undo_ref[which], product)
        mid_ref[pl.ds(2 * group, 2)] = undone.reshape(2, -1, undone.shape[1])

    work(0, 0)

    @pl.loop(1, filter_ref.shape[0])
    def _(group):
        work(group, 1)

    skip = skip_ref[...]
    for pair in range(back_ref.shape[0] // 2):
        sums = jnp.concatenate(
            [last_stage(back_ref, mid_ref, 2 * pair), last_stage(back_ref, mid_ref, 2 * pair + 1)], axis=1
        )
        for part in range(2):
            rows = slice(part * tokens + pair * 2 * SUB, part * tokens + (pair + 1) * 2 * SUB)
            direct = skip * both_ref[:, rows, :].astype(jnp.float32)
            out_ref[:, rows, :] = (sums[:, :, part * LANES : (part + 1) * LANES] + direct).astype(jnp.bfloat16)


def tap_grad_kernel(cross_ref, back_ref, undo_ref, out_ref, mid_ref):
    def work(group, which):
        undone = dot(undo_ref[which], cross_ref[group].astype(jnp.bfloat16))
        mid_ref[pl.ds(2 * group, 2)] = undone.reshape(2, -1, undone.shape[1])

    work(0, 0)

    @pl.loop(1, cross_ref.shape[0])
    def _(group):
        work(group, 1)

    for pair in range(back_ref.shape[0] // 2):
        sums = jnp.concatenate(
            [last_stage(back_ref, mid_ref, 2 * pair), last_stage(back_ref, mid_ref, 2 * pair + 1)], axis=1
        )
        out_ref[:, pair * 2 * SUB : (pair + 1) * 2 * SUB, :] = sums.astype(jnp.bfloat16)


def call(kernel, out_shape, scratch=(), flops=0, moved=0, **grid):
    return pl.pallas_call(
        kernel,
        out_shape=out_shape,
        scratch_shapes=scratch,
        cost_estimate=pl.CostEstimate(flops=flops, bytes_accessed=moved, transcendentals=0),
        compiler_params=pltpu.CompilerParams(vmem_limit_bytes=VMEM_BYTES),
        **grid,
    )


def local(query, key_stream, value_stream, upstream, bases, base_rows, long_filter, skip_weight):
    groups = lax.axis_size("seq")
    tokens, width = query.shape[1:]
    length = tokens * groups
    channels = long_filter.shape[0]
    ahead, back, second, undo = transform_tables(groups, tokens, length ** (-0.5))
    letters = bases.reshape(tokens, 1)
    steps = 8
    per_step = groups // steps
    stream = pl.BlockSpec((None, tokens, width // steps), lambda i: (0, 0, i))
    cols = pl.BlockSpec((per_step, 2 * tokens, channels), lambda i: (i, 0, 0))
    letter_spec = pl.BlockSpec((tokens, 1), lambda i: (0, 0))
    row_spec = pl.BlockSpec((base_rows.shape[0], width // steps), lambda i: (0, i))
    packed = jax.ShapeDtypeStruct((groups, 2 * tokens, channels), jnp.bfloat16)
    array_bytes = tokens * width * 2

    gates = call(
        gate_kernel,
        packed,
        moved=6 * array_bytes,
        grid=(steps,),
        in_specs=[stream, stream, stream, stream, letter_spec, row_spec],
        out_specs=cols,
    )(query, key_stream, value_stream, upstream, letters, base_rows)
    both = lax.all_to_all(gates, "seq", split_axis=0, concat_axis=0, tiled=True)

    all_taps = lax.all_gather(long_filter.T.astype(jnp.bfloat16), "dp", axis=0, tiled=True)
    spectrum_shape = jax.ShapeDtypeStruct((groups, 2 * tokens, channels), jnp.float32)
    one_pass = 2 * 4 * length * 256 * channels
    spectrum = call(
        taps_kernel,
        spectrum_shape,
        [pltpu.VMEM((2 * groups, tokens, channels), jnp.float32)],
        flops=one_pass,
        moved=9 * array_bytes,
    )(all_taps.reshape(groups, tokens, channels), ahead, second)

    out, cross = call(
        main_kernel,
        (packed, spectrum_shape),
        [pltpu.VMEM((2 * groups, tokens, 2 * channels), jnp.float32)],
        flops=4 * one_pass,
        moved=20 * array_bytes,
    )(both, spectrum, skip_weight.reshape(1, channels), ahead, back, second, undo)
    home = lax.all_to_all(out, "seq", split_axis=0, concat_axis=0, tiled=True)

    tap_grad = call(
        tap_grad_kernel,
        jax.ShapeDtypeStruct((groups, tokens, channels), jnp.bfloat16),
        [pltpu.VMEM((2 * groups, tokens, channels), jnp.float32)],
        flops=one_pass,
        moved=9 * array_bytes,
    )(cross, back, undo)
    filter_grad = lax.psum_scatter(
        tap_grad.reshape(length, channels), "dp", scatter_dimension=0, tiled=True
    ).T.astype(jnp.float32)

    grad_shape = jax.ShapeDtypeStruct(query.shape, jnp.bfloat16)
    query_grad, key_grad, value_grad = call(
        ungate_kernel,
        (grad_shape, grad_shape, grad_shape),
        moved=8 * array_bytes,
        grid=(steps,),
        in_specs=[cols, stream, stream, stream, letter_spec, row_spec],
        out_specs=[stream, stream, stream],
    )(home, key_stream, value_stream, upstream, letters, base_rows)
    return (query_grad, key_grad, value_grad, filter_grad)


def solution(mesh):
    return jax.shard_map(
        local,
        mesh=mesh,
        in_specs=(
            P("dp", "seq", None),
            P("dp", "seq", None),
            P("dp", "seq", None),
            P("dp", "seq", None),
            P("dp", "seq"),
            P(),
            P("seq", "dp"),
            P("seq"),
        ),
        out_specs=(
            P("dp", "seq", None),
            P("dp", "seq", None),
            P("dp", "seq", None),
            P("seq", "dp"),
        ),
        check_vma=False,
    )
```

```python
import math

import jax
import jax.numpy as jnp
import ml_dtypes
import numpy as np
from jax import lax
from jax.experimental import pallas as pl
from jax.experimental.pallas import tpu as pltpu
from jax.sharding import PartitionSpec as P

LANES = 128
SUB = 8
PIECES = 8
UNROLL = 8
MEGA = 1024 * 1024
VMEM = pltpu.VMEM
bf16 = jnp.bfloat16


def transform_tables(blocks, rows, scale):
    points = 2 * blocks * rows
    low = 2 * np.arange(blocks)[:, None, None] + 1
    point = np.arange(blocks)[None, None, :] * rows + np.arange(rows)[None, :, None]
    angle = math.pi / points * (low * point % (2 * points))
    first = np.stack([np.cos(angle), -np.sin(angle)], axis=1)
    first = first.reshape(2 * blocks, rows // SUB, SUB, blocks)
    ahead = np.einsum("mhaj,ab->hmajb", first, np.eye(SUB))
    ahead = ahead.reshape(rows // SUB, 2 * blocks * SUB, blocks * SUB)
    back = np.ascontiguousarray(np.swapaxes(ahead, 1, 2))

    row = np.arange(rows)
    angle = 2.0 * math.pi / rows * (row[:, None] * row[None, :] % rows)
    cosine, sine = np.cos(angle), np.sin(angle)
    second = np.block([[cosine, sine], [-sine, cosine]])
    undo = np.ascontiguousarray(second.T) * (2.0 / points * scale)
    return tuple(table.astype(ml_dtypes.bfloat16) for table in (ahead, back, second, undo))


def dot(left, right):
    return jnp.dot(left, right, preferred_element_type=jnp.float32)


def letters_of(bases_ref):
    count = bases_ref.shape[1]
    return jnp.transpose(jnp.broadcast_to(bases_ref[...], (count, count)))


def readout(letters, rows_ref, columns):
    rows = rows_ref[:, columns].astype(jnp.float32)
    picked = rows[0:1]
    for letter in range(1, rows.shape[0]):
        picked = jnp.where(letters == letter, rows[letter : letter + 1], picked)
    return picked


def gate_kernel(query, key, value, upstream, bases_ref, rows_ref, out_ref, held, sems):
    tokens, width = query.shape[1:]
    span = width // PIECES
    copies = []
    for piece in range(PIECES):
        columns = pl.ds(piece * span, span)
        row = []
        for which, source in enumerate((query, key, value, upstream)):
            copy = pltpu.make_async_copy(
                source.at[0, :, columns], held.at[which, :, columns], sems.at[which, piece]
            )
            copy.start()
            row.append(copy)
        copies.append(row)
    letters = letters_of(bases_ref)
    for piece in range(PIECES):
        for copy in copies[piece]:
            copy.wait()
        for block in range(piece * span // LANES, (piece + 1) * span // LANES):
            columns = slice(block * LANES, (block + 1) * LANES)
            query_rows, key_rows, value_rows, upstream_rows = (
                held[which, :, columns].astype(jnp.float32) for which in range(4)
            )
            out_grad = upstream_rows - readout(letters, rows_ref, columns)
            out_ref[block, :tokens, :] = (key_rows * value_rows).astype(bf16)
            out_ref[block, tokens:, :] = (out_grad * query_rows).astype(bf16)


def ungate_kernel(back_ref, key_ref, value_ref, upstream_ref, bases_ref, rows_ref, *rest):
    outs, (held, sems) = rest[:3], rest[3:]
    tokens, width = key_ref.shape[1:]
    span = width // PIECES
    letters = letters_of(bases_ref)
    copies = []
    for piece in range(PIECES):
        for block in range(piece * span // LANES, (piece + 1) * span // LANES):
            columns = slice(block * LANES, (block + 1) * LANES)
            conv = back_ref[block, :tokens, :].astype(jnp.float32)
            corr = back_ref[block, tokens:, :].astype(jnp.float32)
            out_grad = upstream_ref[0, :, columns].astype(jnp.float32) - readout(letters, rows_ref, columns)
            held[0, :, columns] = (out_grad * conv).astype(bf16)
            held[1, :, columns] = (corr * value_ref[0, :, columns].astype(jnp.float32)).astype(bf16)
            held[2, :, columns] = (corr * key_ref[0, :, columns].astype(jnp.float32)).astype(bf16)
        columns = pl.ds(piece * span, span)
        for which, target in enumerate(outs):
            copy = pltpu.make_async_copy(
                held.at[which, :, columns], target.at[0, :, columns], sems.at[which, piece]
            )
            copy.start()
            copies.append(copy)
    for copy in copies:
        copy.wait()


def turn_kernel(in_ref, out_ref):
    wide, high = out_ref.shape[0] // LANES, out_ref.shape[1] // LANES
    for row in range(wide):
        for column in range(high):
            rows, columns = slice(row * LANES, (row + 1) * LANES), slice(column * LANES, (column + 1) * LANES)
            out_ref[rows, columns] = jnp.transpose(in_ref[columns, rows].astype(jnp.float32)).astype(out_ref.dtype)


def first_stage(load, ahead_ref, mid_ref):
    for pair in range(ahead_ref.shape[0] // 2):
        both = load(pair)
        halves = []
        for part in range(2):
            piece = both[:, part * SUB : (part + 1) * SUB, :]
            piece = piece.reshape(piece.shape[0] * SUB, piece.shape[2]).astype(bf16)
            mid = dot(ahead_ref[2 * pair + part], piece)
            halves.append(mid.reshape(-1, SUB, mid.shape[1]))
        mid_ref[:, pair * 2 * SUB : (pair + 1) * 2 * SUB, :] = jnp.concatenate(halves, axis=1).astype(bf16)


def last_stage(back_ref, wide_ref, pair):
    halves = []
    for step in (2 * pair, 2 * pair + 1):
        piece = wide_ref[:, step * SUB : (step + 1) * SUB, :]
        piece = piece.reshape(piece.shape[0] * SUB, piece.shape[2]).astype(bf16)
        out = dot(back_ref[step], piece)
        halves.append(out.reshape(-1, SUB, out.shape[1]))
    return jnp.concatenate(halves, axis=1)


def for_groups(count, work):
    @pl.loop(0, count // UNROLL)
    def _(turn):
        for step in range(UNROLL):
            work(turn * UNROLL + step)


def group_of(ref, group):
    both = ref[pl.ds(2 * group, 2)]
    return both.reshape(2 * both.shape[1], both.shape[2])


def taps_kernel(taps_ref, ahead_ref, second_ref, spectrum_ref, mid_ref):
    def load(pair):
        return taps_ref[:, pair * 2 * SUB : (pair + 1) * 2 * SUB, :].astype(jnp.float32)

    first_stage(load, ahead_ref, mid_ref)

    def work(group):
        spectrum_ref[group] = dot(second_ref[...], group_of(mid_ref, group))

    for_groups(spectrum_ref.shape[0], work)


def times(left, right, conjugate):
    half = left.shape[0] // 2
    left_real, left_imag = left[:half], left[half:]
    right_real, right_imag = right[:half], right[half:]
    if conjugate:
        real = left_real * right_real + left_imag * right_imag
        imag = left_imag * right_real - left_real * right_imag
    else:
        real = left_real * right_real - left_imag * right_imag
        imag = left_imag * right_real + left_real * right_imag
    return jnp.concatenate([real, imag], axis=0)


def main_kernel(
    both_ref, filter_ref, skip_ref, ahead_ref, back_ref, second_ref, undo_ref, out_ref, cross_ref, mid_ref, wide_ref
):
    tokens = both_ref.shape[1] // 2

    def load(pair):
        rows = slice(pair * 2 * SUB, (pair + 1) * 2 * SUB)
        more = slice(tokens + pair * 2 * SUB, tokens + (pair + 1) * 2 * SUB)
        return jnp.concatenate([both_ref[:, rows, :], both_ref[:, more, :]], axis=2).astype(jnp.float32)

    first_stage(load, ahead_ref, mid_ref)

    def work(group):
        spectrum = dot(second_ref[...], group_of(mid_ref, group))
        gated, grad = spectrum[:, :LANES], spectrum[:, LANES:]
        taps = filter_ref[group]
        conv = times(gated, taps, False)
        corr = times(grad, taps, True)
        cross_ref[group] = times(grad, gated, True).astype(bf16)
        undone = dot(undo_ref[...], jnp.concatenate([conv, corr], axis=1).astype(bf16))
        wide_ref[pl.ds(2 * group, 2)] = undone.reshape(2, -1, undone.shape[1])

    for_groups(filter_ref.shape[0], work)

    skip = skip_ref[...]
    for pair in range(back_ref.shape[0] // 2):
        sums = last_stage(back_ref, wide_ref, pair)
        for part in range(2):
            rows = slice(part * tokens + pair * 2 * SUB, part * tokens + (pair + 1) * 2 * SUB)
            direct = skip * both_ref[:, rows, :].astype(jnp.float32)
            out_ref[:, rows, :] = (sums[:, :, part * LANES : (part + 1) * LANES] + direct).astype(bf16)


def tap_grad_kernel(cross_ref, back_ref, undo_ref, out_ref, wide_ref):
    def work(group):
        undone = dot(undo_ref[...], cross_ref[group])
        wide_ref[pl.ds(2 * group, 2)] = undone.reshape(2, -1, undone.shape[1])

    for_groups(cross_ref.shape[0], work)
    for pair in range(back_ref.shape[0] // 2):
        out_ref[:, pair * 2 * SUB : (pair + 1) * 2 * SUB, :] = last_stage(back_ref, wide_ref, pair).astype(bf16)


def call(kernel, args, outs, scratch, limit, far=(), flops=0, moved=0):
    args = [
        pltpu.with_memory_space_constraint(arg, pltpu.HBM if place in far else VMEM) for place, arg in enumerate(args)
    ]
    in_specs = [pl.BlockSpec(memory_space=pl.ANY if place in far else VMEM) for place in range(len(args))]
    near = [isinstance(out, jax.ShapeDtypeStruct) for out in outs]
    return pl.pallas_call(
        kernel,
        out_shape=tuple(out if plain else VMEM(*out) for out, plain in zip(outs, near)),
        in_specs=in_specs,
        out_specs=tuple(pl.BlockSpec(memory_space=pl.ANY if plain else VMEM) for plain in near),
        scratch_shapes=scratch,
        cost_estimate=pl.CostEstimate(flops=flops, bytes_accessed=moved, transcendentals=0),
        compiler_params=pltpu.CompilerParams(vmem_limit_bytes=limit * MEGA),
    )(*args)


def local(query, key_stream, value_stream, upstream, bases, base_rows, long_filter, skip_weight):
    groups = lax.axis_size("seq")
    tokens, width = query.shape[1:]
    length = tokens * groups
    channels = long_filter.shape[0]
    ahead, back, second, undo = transform_tables(groups, tokens, length ** (-0.5))
    packed = ((groups, 2 * tokens, channels), bf16)
    array_bytes = tokens * width * 2

    (turned,) = call(turn_kernel, (long_filter,), [(long_filter.shape[::-1], bf16)], [], 4)
    all_taps = lax.all_gather(turned, "dp", axis=0, tiled=True)
    (gates,) = call(
        gate_kernel,
        (query, key_stream, value_stream, upstream, bases, base_rows),
        [packed],
        [VMEM((4, tokens, width), bf16), pltpu.SemaphoreType.DMA((4, PIECES))],
        12,
        far=(0, 1, 2, 3),
        moved=6 * array_bytes,
    )
    both = lax.all_to_all(gates, "seq", split_axis=0, concat_axis=0, tiled=True)

    one_pass = 2 * 4 * length * 256 * channels
    (spectrum,) = call(
        taps_kernel,
        (all_taps.reshape(groups, tokens, channels), ahead, second),
        [((groups, 2 * tokens, channels), jnp.float32)],
        [VMEM((2 * groups, tokens, channels), bf16)],
        8,
        flops=one_pass,
        moved=array_bytes,
    )
    out, cross = call(
        main_kernel,
        (both, spectrum, skip_weight.reshape(1, channels), ahead, back, second, undo),
        [packed, packed],
        [VMEM((2 * groups, tokens, 2 * channels), bf16), VMEM((2 * groups, tokens, 2 * channels), jnp.float32)],
        20,
        flops=4 * one_pass,
        moved=array_bytes,
    )
    home = lax.all_to_all(out, "seq", split_axis=0, concat_axis=0, tiled=True)

    (tap_grad,) = call(
        tap_grad_kernel,
        (cross, back, undo),
        [((groups, tokens, channels), bf16)],
        [VMEM((2 * groups, tokens, channels), jnp.float32)],
        10,
        flops=one_pass,
        moved=array_bytes,
    )
    summed = lax.psum_scatter(tap_grad.reshape(length, channels), "dp", scatter_dimension=0, tiled=True)
    (filter_grad,) = call(turn_kernel, (summed,), [(long_filter.shape, jnp.float32)], [], 4)

    grad_shape = jax.ShapeDtypeStruct(query.shape, bf16)
    query_grad, key_grad, value_grad = call(
        ungate_kernel,
        (home, key_stream, value_stream, upstream, bases, base_rows),
        [grad_shape, grad_shape, grad_shape],
        [VMEM((3, tokens, width), bf16), pltpu.SemaphoreType.DMA((3, PIECES))],
        12,
        moved=6 * array_bytes,
    )
    return (query_grad, key_grad, value_grad, filter_grad)


def solution(mesh):
    return jax.shard_map(
        local,
        mesh=mesh,
        in_specs=(
            P("dp", "seq", None),
            P("dp", "seq", None),
            P("dp", "seq", None),
            P("dp", "seq", None),
            P("dp", "seq"),
            P(),
            P("seq", "dp"),
            P("seq"),
        ),
        out_specs=(
            P("dp", "seq", None),
            P("dp", "seq", None),
            P("dp", "seq", None),
            P("seq", "dp"),
        ),
        check_vma=False,
    )
```

```python
import math

import jax
import jax.numpy as jnp
import ml_dtypes
import numpy as np
from jax import lax
from jax.experimental import pallas as pl
from jax.experimental.pallas import tpu as pltpu
from jax.sharding import PartitionSpec as P

LANES = 128
SUB = 8
PIECES = 8
UNROLL = 8
TABLE_PIECES = 4
Z_PAIRS = 2
Y_PLACES = 4
TAP_BLOCKS = 4
MEGA = 1024 * 1024
VMEM = pltpu.VMEM
bf16 = jnp.bfloat16


def transform_tables(blocks, rows, scale):
    points = 2 * blocks * rows
    low = 2 * np.arange(blocks)[:, None, None] + 1
    point = np.arange(blocks)[None, None, :] * rows + np.arange(rows)[None, :, None]
    angle = math.pi / points * (low * point % (2 * points))
    first = np.stack([np.cos(angle), -np.sin(angle)], axis=1)
    first = first.reshape(2 * blocks, rows // SUB, SUB, blocks)
    ahead = np.einsum("mhaj,ab->hmajb", first, np.eye(SUB))
    ahead = ahead.reshape(rows // SUB, 2 * blocks * SUB, blocks * SUB)
    back = np.ascontiguousarray(np.swapaxes(ahead, 1, 2))

    row = np.arange(rows)
    angle = 2.0 * math.pi / rows * (row[:, None] * row[None, :] % rows)
    cosine, sine = np.cos(angle), np.sin(angle)
    second = np.block([[cosine, sine], [-sine, cosine]])
    undo = np.ascontiguousarray(second.T) * (2.0 / points * scale)
    return tuple(table.astype(ml_dtypes.bfloat16) for table in (ahead, back, second, undo))


def dot(left, right):
    return jnp.dot(left, right, preferred_element_type=jnp.float32)


def letters_of(bases_ref):
    count = bases_ref.shape[1]
    return jnp.transpose(jnp.broadcast_to(bases_ref[...], (count, count)))


def readout(letters, rows_ref, columns):
    rows = rows_ref[:, columns].astype(jnp.float32)
    picked = rows[0:1]
    for letter in range(1, rows.shape[0]):
        picked = jnp.where(letters == letter, rows[letter : letter + 1], picked)
    return picked


def gate_kernel(query, key, value, upstream, bases_ref, rows_ref, out_ref, held, sems):
    tokens, width = query.shape[1:]
    span = width // PIECES
    copies = []
    for piece in range(PIECES):
        columns = pl.ds(piece * span, span)
        row = []
        for which, source in enumerate((query, key, value, upstream)):
            copy = pltpu.make_async_copy(
                source.at[0, :, columns], held.at[which, :, columns], sems.at[which, piece]
            )
            copy.start()
            row.append(copy)
        copies.append(row)
    letters = letters_of(bases_ref)
    for piece in range(PIECES):
        for copy in copies[piece]:
            copy.wait()
        for block in range(piece * span // LANES, (piece + 1) * span // LANES):
            columns = slice(block * LANES, (block + 1) * LANES)
            query_rows, key_rows, value_rows, upstream_rows = (
                held[which, :, columns].astype(jnp.float32) for which in range(4)
            )
            out_grad = upstream_rows - readout(letters, rows_ref, columns)
            out_ref[block, :tokens, :] = (key_rows * value_rows).astype(bf16)
            out_ref[block, tokens:, :] = (out_grad * query_rows).astype(bf16)


def ungate_kernel(back_ref, key, value, upstream, bases_ref, rows_ref, *rest):
    outs, (held, in_sems, made, out_sems) = rest[:3], rest[3:]
    tokens, width = key.shape[1:]
    span = width // PIECES
    arriving = []
    for piece in range(PIECES):
        columns = pl.ds(piece * span, span)
        row = []
        for which, source in enumerate((key, value, upstream)):
            copy = pltpu.make_async_copy(
                source.at[0, :, columns], held.at[which, :, columns], in_sems.at[which, piece]
            )
            copy.start()
            row.append(copy)
        arriving.append(row)
    letters = letters_of(bases_ref)
    leaving = []
    for piece in range(PIECES):
        for copy in arriving[piece]:
            copy.wait()
        for block in range(piece * span // LANES, (piece + 1) * span // LANES):
            columns = slice(block * LANES, (block + 1) * LANES)
            conv = back_ref[block, :tokens, :].astype(jnp.float32)
            corr = back_ref[block, tokens:, :].astype(jnp.float32)
            key_rows, value_rows, upstream_rows = (held[which, :, columns].astype(jnp.float32) for which in range(3))
            out_grad = upstream_rows - readout(letters, rows_ref, columns)
            made[0, :, columns] = (out_grad * conv).astype(bf16)
            made[1, :, columns] = (corr * value_rows).astype(bf16)
            made[2, :, columns] = (corr * key_rows).astype(bf16)
        columns = pl.ds(piece * span, span)
        for which, target in enumerate(outs):
            copy = pltpu.make_async_copy(
                made.at[which, :, columns], target.at[0, :, columns], out_sems.at[which, piece]
            )
            copy.start()
            leaving.append(copy)
    for copy in leaving:
        copy.wait()


def turn_kernel(in_ref, out_ref):
    blocks, rows, channels = out_ref.shape
    for block in range(blocks):
        out_ref[block] = jnp.transpose(in_ref[:, block * rows : (block + 1) * rows]).astype(bf16)


def first_stage(load, table, mid_ref):
    for pair in range(mid_ref.shape[1] // (2 * SUB)):
        both = load(pair)
        halves = []
        for part in range(2):
            piece = both[:, part * SUB : (part + 1) * SUB, :]
            piece = piece.reshape(piece.shape[0] * SUB, piece.shape[2]).astype(bf16)
            mid = dot(table(2 * pair + part), piece)
            halves.append(mid.reshape(-1, SUB, mid.shape[1]))
        mid_ref[:, pair * 2 * SUB : (pair + 1) * 2 * SUB, :] = jnp.concatenate(halves, axis=1).astype(bf16)


def last_stage(table, wide_ref, pair):
    halves = []
    for step in (2 * pair, 2 * pair + 1):
        piece = wide_ref[:, step * SUB : (step + 1) * SUB, :]
        piece = piece.reshape(piece.shape[0] * SUB, piece.shape[2]).astype(bf16)
        out = dot(table(step), piece)
        halves.append(out.reshape(-1, SUB, out.shape[1]))
    return jnp.concatenate(halves, axis=1)


def for_groups(count, work):
    @pl.loop(0, count // UNROLL)
    def _(turn):
        for step in range(UNROLL):
            work(turn * UNROLL + step)


def group_of(ref, group):
    both = ref[pl.ds(2 * group, 2)]
    return both.reshape(2 * both.shape[1], both.shape[2])


def times(left, right, conjugate):
    half = left.shape[0] // 2
    left_real, left_imag = left[:half], left[half:]
    right_real, right_imag = right[:half], right[half:]
    if conjugate:
        real = left_real * right_real + left_imag * right_imag
        imag = left_imag * right_real - left_real * right_imag
    else:
        real = left_real * right_real - left_imag * right_imag
        imag = left_imag * right_real + left_real * right_imag
    return jnp.concatenate([real, imag], axis=0)


def place():
    index = lax.axis_index("dp")
    return index // Y_PLACES, lax.rem(index, Y_PLACES)


def block_of(pair, turn):
    pair_here, place_here = place()
    owner = lax.rem(pair_here + pair, Z_PAIRS) * Y_PLACES + lax.rem(place_here + turn + Y_PLACES, Y_PLACES)
    return pl.ds(owner * TAP_BLOCKS, TAP_BLOCKS)


def middle_kernel(both_ref, *refs):
    taps_hbm, refs = refs[:Y_PLACES], refs[Y_PLACES:]
    (skip_ref, ahead_hbm, back_hbm, second_ref, undo_ref, out_ref), refs = refs[:6], refs[6:]
    tap_outs, refs = refs[:Y_PLACES], refs[Y_PLACES:]
    taps_ref, ahead_ref, back_ref, tap_mid_ref, mid_ref, spectrum_ref, cross_ref, wide_ref = refs[:8]
    taps_sems, ahead_sems, back_sems, out_sems = refs[8:]
    groups = both_ref.shape[0]
    tokens = both_ref.shape[1] // 2
    steps = ahead_ref.shape[0]
    pairs = steps // 2

    def chunk(pair):
        return slice(pair * 2 * SUB, (pair + 1) * 2 * SUB)

    tap_copies = []
    for turn in range(Y_PLACES):
        for pair in range(Z_PAIRS):
            target = taps_ref.at[block_of(pair, -turn)]
            tap_copies.append(pltpu.make_async_copy(taps_hbm[turn].at[pair], target, taps_sems.at[turn, pair]))
            tap_copies[-1].start()
    span = steps // TABLE_PIECES
    ahead_copies = []
    back_copies = []
    for source, target, sems, copies in (
        (ahead_hbm, ahead_ref, ahead_sems, ahead_copies),
        (back_hbm, back_ref, back_sems, back_copies),
    ):
        for piece in range(TABLE_PIECES):
            rows = pl.ds(piece * span, span)
            copies.append(pltpu.make_async_copy(source.at[rows], target.at[rows], sems.at[piece]))
            copies[-1].start()

    for copy in tap_copies:
        copy.wait()

    def load_taps(pair):
        return taps_ref[:, chunk(pair), :].astype(jnp.float32)

    def fresh_ahead(step):
        if step % span == 0:
            ahead_copies[step // span].wait()
        return ahead_ref[step]

    first_stage(load_taps, fresh_ahead, tap_mid_ref)

    def transform_taps(group):
        spectrum_ref[group] = dot(second_ref[...], group_of(tap_mid_ref, group))

    for_groups(groups, transform_taps)

    def load_both(pair):
        rows = chunk(pair)
        more = slice(tokens + rows.start, tokens + rows.stop)
        return jnp.concatenate([both_ref[:, rows, :], both_ref[:, more, :]], axis=2).astype(jnp.float32)

    first_stage(load_both, lambda step: ahead_ref[step], mid_ref)

    def work(group):
        spectrum = dot(second_ref[...], group_of(mid_ref, group))
        gated, grad = spectrum[:, :LANES], spectrum[:, LANES:]
        taps = spectrum_ref[group]
        conv = times(gated, taps, False)
        corr = times(grad, taps, True)
        cross_ref[group] = times(grad, gated, True).astype(bf16)
        undone = dot(undo_ref[...], jnp.concatenate([conv, corr], axis=1).astype(bf16))
        wide_ref[pl.ds(2 * group, 2)] = undone.reshape(2, -1, undone.shape[1])

    for_groups(groups, work)

    for copy in back_copies:
        copy.wait()

    def back_table(step):
        return back_ref[step]

    skip = skip_ref[...]
    for pair in range(pairs):
        sums = last_stage(back_table, wide_ref, pair)
        for part in range(2):
            rows = slice(part * tokens + pair * 2 * SUB, part * tokens + (pair + 1) * 2 * SUB)
            direct = skip * both_ref[:, rows, :].astype(jnp.float32)
            out_ref[:, rows, :] = (sums[:, :, part * LANES : (part + 1) * LANES] + direct).astype(bf16)

    def undo_cross(group):
        undone = dot(undo_ref[...], cross_ref[group])
        spectrum_wide[pl.ds(2 * group, 2)] = undone.reshape(2, -1, undone.shape[1])

    spectrum_wide = wide_ref.at[:, :, :LANES]
    for_groups(groups, undo_cross)
    for pair in range(pairs):
        taps_ref[:, chunk(pair), :] = last_stage(back_table, spectrum_wide, pair).astype(bf16)

    leaving = []
    for turn in range(Y_PLACES):
        for pair in range(Z_PAIRS):
            source = taps_ref.at[block_of(pair, turn)]
            leaving.append(pltpu.make_async_copy(source, tap_outs[turn].at[pair], out_sems.at[turn, pair]))
            leaving[-1].start()
    for copy in leaving:
        copy.wait()


def join_kernel(*refs):
    parts, (kept_ref, sent_ref) = refs[:-2], refs[-2:]
    total = parts[0][...].astype(jnp.float32)
    for part in parts[1:]:
        total = total + part[...].astype(jnp.float32)
    kept_ref[...] = total[0]
    sent_ref[...] = total[1].astype(bf16)


def finish_kernel(kept_ref, came_ref, out_ref):
    blocks, rows, channels = kept_ref.shape
    for block in range(blocks):
        total = kept_ref[block] + came_ref[block].astype(jnp.float32)
        out_ref[:, block * rows : (block + 1) * rows] = jnp.transpose(total)


def call(kernel, args, outs, scratch, limit, flops=0, moved=0):
    in_specs = []
    held = []
    for arg, space in args:
        held.append(arg if space in (None, pl.ANY) else pltpu.with_memory_space_constraint(arg, space))
        in_specs.append(pl.BlockSpec(memory_space=pl.ANY if space in (pl.ANY, pltpu.HBM) else VMEM))
    out_shape = []
    out_specs = []
    for shape, dtype, space in outs:
        out_shape.append(jax.ShapeDtypeStruct(shape, dtype) if space is None else space(shape, dtype))
        out_specs.append(pl.BlockSpec(memory_space=pl.ANY if space is pltpu.HBM else VMEM))
    return pl.pallas_call(
        kernel,
        out_shape=tuple(out_shape),
        in_specs=in_specs,
        out_specs=tuple(out_specs),
        scratch_shapes=scratch,
        cost_estimate=pl.CostEstimate(flops=flops, bytes_accessed=moved, transcendentals=0),
        compiler_params=pltpu.CompilerParams(vmem_limit_bytes=limit * MEGA),
    )(*held)


def along_dp(array, pairs, places):
    sources = [(pair, place) for pair in range(Z_PAIRS) for place in range(Y_PLACES)]
    moves = [
        (pair * Y_PLACES + place, (pair + pairs) % Z_PAIRS * Y_PLACES + (place + places) % Y_PLACES)
        for pair, place in sources
    ]
    return lax.ppermute(array, "dp", moves)


def exchange(array):
    always = lax.optimization_barrier(jnp.int32(1)) == 1
    return lax.cond(
        always,
        lambda whole: lax.all_to_all(whole, "seq", split_axis=0, concat_axis=0, tiled=True),
        lambda whole: whole,
        array,
    )


def local(query, key_stream, value_stream, upstream, bases, base_rows, long_filter, skip_weight):
    groups = lax.axis_size("seq")
    tokens, width = query.shape[1:]
    length = tokens * groups
    channels = long_filter.shape[0]
    ahead, back, second, undo = (jnp.asarray(table) for table in transform_tables(groups, tokens, length ** (-0.5)))
    array_bytes = tokens * width * 2
    far, free, dma = pltpu.HBM, None, pltpu.SemaphoreType.DMA
    steps = ahead.shape[0]
    packed = ((groups, 2 * tokens, channels), bf16, VMEM)
    tap_block = (TAP_BLOCKS, tokens, channels)
    tap_pair = ((Z_PAIRS,) + tap_block, bf16, far)

    (turned,) = call(turn_kernel, [(long_filter, free)], [(tap_block, bf16, free)], [], 4)
    other = along_dp(turned, 1, 0)
    (gates,) = call(
        gate_kernel,
        [(query, far), (key_stream, far), (value_stream, far), (upstream, far), (bases, free), (base_rows, free)],
        [packed],
        [VMEM((4, tokens, width), bf16), dma((4, PIECES))],
        12,
        moved=6 * array_bytes,
    )
    gates, own_taps = lax.optimization_barrier((gates, jnp.stack([turned, other])))
    taps = [own_taps] + [along_dp(own_taps, 0, turn) for turn in range(1, Y_PLACES)]
    both = exchange(gates)

    half_mid = (2 * groups, tokens, channels)
    wide_mid = (2 * groups, tokens, 2 * channels)
    spectra = (groups, 2 * tokens, channels)
    out, *tap_grads = call(
        middle_kernel,
        [(both, VMEM)]
        + [(part, pl.ANY) for part in taps]
        + [
            (skip_weight.reshape(1, channels), free),
            (ahead, far),
            (back, far),
            (second, free),
            (undo, free),
        ],
        [packed] + [tap_pair] * Y_PLACES,
        [
            VMEM((groups, tokens, channels), bf16),
            VMEM(ahead.shape, bf16),
            VMEM(back.shape, bf16),
            VMEM(half_mid, bf16),
            VMEM(wide_mid, bf16),
            VMEM(spectra, jnp.float32),
            VMEM(spectra, bf16),
            VMEM(wide_mid, jnp.float32),
            dma((Y_PLACES, Z_PAIRS)),
            dma((TABLE_PIECES,)),
            dma((TABLE_PIECES,)),
            dma((Y_PLACES, Z_PAIRS)),
        ],
        40,
        flops=2 * 24 * length * 256 * channels,
        moved=12 * array_bytes,
    )
    came = [along_dp(tap_grads[turn], 0, turn) for turn in range(1, Y_PLACES)]
    home, *came = lax.optimization_barrier((exchange(out), *came))

    kept, sent = call(
        join_kernel,
        [(part, free) for part in [tap_grads[0]] + came],
        [(tap_block, jnp.float32, free), (tap_block, bf16, free)],
        [],
        8,
    )
    last = along_dp(sent, 1, 0)
    grad = (query.shape, bf16, far)
    query_grad, key_grad, value_grad = call(
        ungate_kernel,
        [(home, VMEM), (key_stream, far), (value_stream, far), (upstream, far), (bases, free), (base_rows, free)],
        [grad, grad, grad],
        [
            VMEM((3, tokens, width), bf16),
            dma((3, PIECES)),
            VMEM((3, tokens, width), bf16),
            dma((3, PIECES)),
        ],
        16,
        moved=6 * array_bytes,
    )
    (filter_grad,) = call(finish_kernel, [(kept, free), (last, free)], [(long_filter.shape, jnp.float32, free)], [], 8)
    return (query_grad, key_grad, value_grad, filter_grad)


def solution(mesh):
    return jax.shard_map(
        local,
        mesh=mesh,
        in_specs=(
            P("dp", "seq", None),
            P("dp", "seq", None),
            P("dp", "seq", None),
            P("dp", "seq", None),
            P("dp", "seq"),
            P(),
            P("seq", "dp"),
            P("seq"),
        ),
        out_specs=(
            P("dp", "seq", None),
            P("dp", "seq", None),
            P("dp", "seq", None),
            P("seq", "dp"),
        ),
        check_vma=False,
    )
```

```python
import math

import jax
import jax.numpy as jnp
import ml_dtypes
import numpy as np
from jax import lax
from jax.experimental import pallas as pl
from jax.experimental.pallas import tpu as pltpu
from jax.sharding import PartitionSpec as P

LANES = 128
SUB = 8
PIECES = 8
Z_PAIRS = 2
Y_PLACES = 4
TAP_BLOCKS = 4
TABLE_PIECES = 2
MEGA = 1024 * 1024
VMEM = pltpu.VMEM
bf16 = jnp.bfloat16


def transform_tables(blocks, rows, scale):
    points = 2 * blocks * rows
    low = 2 * np.arange(blocks)[:, None, None] + 1
    point = np.arange(blocks)[None, None, :] * rows + np.arange(rows)[None, :, None]
    angle = math.pi / points * (low * point % (2 * points))
    first = np.stack([np.cos(angle), -np.sin(angle)], axis=1)
    first = first.reshape(2 * blocks, rows // SUB, SUB, blocks)
    ahead = np.einsum("mhaj,ab->hmajb", first, np.eye(SUB))
    ahead = ahead.reshape(rows // SUB, 2 * blocks * SUB, blocks * SUB)
    back = np.ascontiguousarray(np.swapaxes(ahead, 1, 2))

    row = np.arange(rows)
    angle = 2.0 * math.pi / rows * (row[:, None] * row[None, :] % rows)
    cosine, sine = np.cos(angle), np.sin(angle)
    second = np.block([[cosine, sine], [-sine, cosine]])
    undo = np.ascontiguousarray(second.T) * (2.0 / points * scale)
    return tuple(table.astype(ml_dtypes.bfloat16) for table in (ahead, back, second, undo))


def dot(left, right):
    return jnp.dot(left, right, preferred_element_type=jnp.float32)


def letters_of(bases_ref):
    count = bases_ref.shape[1]
    return jnp.transpose(jnp.broadcast_to(bases_ref[...], (count, count)))


def readout(letters, rows_ref, columns):
    rows = rows_ref[:, columns].astype(jnp.float32)
    picked = rows[0:1]
    for letter in range(1, rows.shape[0]):
        picked = jnp.where(letters == letter, rows[letter : letter + 1], picked)
    return picked


def gate_kernel(query, key, value, upstream, bases, rows, out_ref, held, bases_ref, rows_ref, sems, small_sems):
    tokens, width = query.shape[1:]
    small = [
        pltpu.make_async_copy(bases, bases_ref, small_sems.at[0]),
        pltpu.make_async_copy(rows, rows_ref, small_sems.at[1]),
    ]
    for copy in small:
        copy.start()
    span = width // PIECES
    copies = []
    for piece in range(PIECES):
        columns = pl.ds(piece * span, span)
        row = []
        for which, source in enumerate((query, key, value, upstream)):
            copy = pltpu.make_async_copy(
                source.at[0, :, columns], held.at[which, :, columns], sems.at[which, piece]
            )
            copy.start()
            row.append(copy)
        copies.append(row)
    for copy in small:
        copy.wait()
    letters = letters_of(bases_ref)
    for piece in range(PIECES):
        for copy in copies[piece]:
            copy.wait()
        for block in range(piece * span // LANES, (piece + 1) * span // LANES):
            columns = slice(block * LANES, (block + 1) * LANES)
            query_rows, key_rows, value_rows, upstream_rows = (
                held[which, :, columns].astype(jnp.float32) for which in range(4)
            )
            out_grad = upstream_rows - readout(letters, rows_ref, columns)
            out_ref[block, :tokens, :] = (key_rows * value_rows).astype(bf16)
            out_ref[block, tokens:, :] = (out_grad * query_rows).astype(bf16)


def ungate_kernel(back_ref, key, value, upstream, bases_ref, rows_ref, *rest):
    outs, (held, in_sems, made, out_sems) = rest[:3], rest[3:]
    tokens, width = key.shape[1:]
    span = width // PIECES
    arriving = []
    for piece in range(PIECES):
        columns = pl.ds(piece * span, span)
        row = []
        for which, source in enumerate((key, value, upstream)):
            copy = pltpu.make_async_copy(
                source.at[0, :, columns], held.at[which, :, columns], in_sems.at[which, piece]
            )
            copy.start()
            row.append(copy)
        arriving.append(row)
    letters = letters_of(bases_ref)
    leaving = []
    for piece in range(PIECES):
        for copy in arriving[piece]:
            copy.wait()
        for block in range(piece * span // LANES, (piece + 1) * span // LANES):
            columns = slice(block * LANES, (block + 1) * LANES)
            conv = back_ref[block, :tokens, :].astype(jnp.float32)
            corr = back_ref[block, tokens:, :].astype(jnp.float32)
            key_rows, value_rows, upstream_rows = (held[which, :, columns].astype(jnp.float32) for which in range(3))
            out_grad = upstream_rows - readout(letters, rows_ref, columns)
            made[0, :, columns] = (out_grad * conv).astype(bf16)
            made[1, :, columns] = (corr * value_rows).astype(bf16)
            made[2, :, columns] = (corr * key_rows).astype(bf16)
        columns = pl.ds(piece * span, span)
        for which, target in enumerate(outs):
            copy = pltpu.make_async_copy(
                made.at[which, :, columns], target.at[0, :, columns], out_sems.at[which, piece]
            )
            copy.start()
            leaving.append(copy)
    for copy in leaving:
        copy.wait()


def turn_kernel(taps_hbm, out_ref, held, sems):
    copies = []
    for block in range(held.shape[0]):
        columns = pl.ds(block * LANES, LANES)
        copies.append(pltpu.make_async_copy(taps_hbm.at[:, columns], held.at[block], sems.at[block]))
        copies[-1].start()
    for block, copy in enumerate(copies):
        copy.wait()
        out_ref[block] = jnp.transpose(held[block]).astype(bf16)


def chunk(pair, first=0):
    return slice(first + pair * 2 * SUB, first + (pair + 1) * 2 * SUB)


def first_stage(load, table, mid_ref):
    for pair in range(mid_ref.shape[1] // (2 * SUB)):
        both = load(pair)
        halves = []
        for part in range(2):
            piece = both[:, part * SUB : (part + 1) * SUB, :]
            piece = piece.reshape(piece.shape[0] * SUB, piece.shape[2]).astype(bf16)
            mid = dot(table(2 * pair + part), piece)
            halves.append(mid.reshape(-1, SUB, mid.shape[1]))
        mid_ref[:, chunk(pair), :] = jnp.concatenate(halves, axis=1).astype(bf16)


def last_stage(table, wide_ref, pair):
    halves = []
    for step in (2 * pair, 2 * pair + 1):
        piece = wide_ref[:, step * SUB : (step + 1) * SUB, :]
        piece = piece.reshape(piece.shape[0] * SUB, piece.shape[2]).astype(bf16)
        out = dot(table(step), piece)
        halves.append(out.reshape(-1, SUB, out.shape[1]))
    return jnp.concatenate(halves, axis=1)


def times(left, right, conjugate):
    half = left.shape[0] // 2
    left_real, left_imag = left[:half], left[half:]
    right_real, right_imag = right[:half], right[half:]
    if conjugate:
        real = left_real * right_real + left_imag * right_imag
        imag = left_imag * right_real - left_real * right_imag
    else:
        real = left_real * right_real - left_imag * right_imag
        imag = left_imag * right_real + left_real * right_imag
    return jnp.concatenate([real, imag], axis=0)


def place():
    index = lax.axis_index("dp")
    return index // Y_PLACES, lax.rem(index, Y_PLACES)


def place_at(turn):
    return lax.rem(place()[1] + turn + Y_PLACES, Y_PLACES)


def middle_kernel(both_hbm, *refs):
    taps_hbm, refs = refs[:Y_PLACES], refs[Y_PLACES:]
    (skip_ref, ahead_hbm, back_hbm, second_ref, undo_ref, out_ref), refs = refs[:6], refs[6:]
    tap_outs, refs = refs[:Y_PLACES], refs[Y_PLACES:]
    both_ref, taps_ref, mid_ref, wide_ref, ahead_ref, back_ref = refs[:6]
    both_sem, taps_sems, out_sems, ahead_sems, back_sem = refs[6:]
    groups = both_ref.shape[0]
    tokens = both_ref.shape[1] // 2
    steps = ahead_ref.shape[0]
    span = steps // TABLE_PIECES
    ahead_copies = []
    for piece in range(TABLE_PIECES):
        rows = pl.ds(piece * span, span)
        ahead_copies.append(pltpu.make_async_copy(ahead_hbm.at[rows], ahead_ref.at[rows], ahead_sems.at[piece]))
    back_copy = pltpu.make_async_copy(back_hbm, back_ref, back_sem)
    ahead_copies[0].start()
    arriving = [pltpu.make_async_copy(both_hbm, both_ref, both_sem)]
    arriving[-1].start()
    for turn in range(Y_PLACES):
        arriving.append(
            pltpu.make_async_copy(taps_hbm[turn], taps_ref.at[:, place_at(-turn)], taps_sems.at[turn])
        )
        arriving[-1].start()
    for copy in ahead_copies[1:] + [back_copy]:
        copy.start()
    for copy in arriving:
        copy.wait()

    def load(pair):
        filt = taps_ref[:, :, :, chunk(pair), :].reshape(groups, 2 * SUB, LANES)
        parts = [both_ref[:, chunk(pair), :], both_ref[:, chunk(pair, tokens), :], filt]
        return jnp.concatenate(parts, axis=2).astype(jnp.float32)

    def fresh_ahead(step):
        if step % span == 0:
            ahead_copies[step // span].wait()
        return ahead_ref[step]

    first_stage(load, fresh_ahead, mid_ref)

    def group_of(group, columns):
        both = mid_ref[2 * group : 2 * group + 2, :, columns]
        return both.reshape(2 * tokens, both.shape[2])

    second, undo = second_ref[...], undo_ref[...]
    signals, taps = slice(0, 2 * LANES), slice(2 * LANES, 3 * LANES)
    for pair in range(groups // 2):
        here = (2 * pair, 2 * pair + 1)
        filters = dot(second, jnp.concatenate([group_of(group, taps) for group in here], axis=1))
        crosses = []
        for which, group in enumerate(here):
            spectrum = dot(second, group_of(group, signals))
            gated, grad = spectrum[:, :LANES], spectrum[:, LANES:]
            filt = filters[:, which * LANES : (which + 1) * LANES]
            product = jnp.concatenate([times(gated, filt, False), times(grad, filt, True)], axis=1)
            undone = dot(undo, product.astype(bf16))
            wide_ref[2 * group : 2 * group + 2, :, signals] = undone.reshape(2, tokens, 2 * LANES)
            crosses.append(times(grad, gated, True))
        undone = dot(undo, jnp.concatenate(crosses, axis=1).astype(bf16))
        for which, group in enumerate(here):
            part = undone[:, which * LANES : (which + 1) * LANES]
            wide_ref[2 * group : 2 * group + 2, :, taps] = part.reshape(2, tokens, LANES)

    skip = skip_ref[...]

    back_copy.wait()

    for pair in range(steps // 2):
        sums = last_stage(lambda step: back_ref[step], wide_ref, pair)
        for part in range(2):
            rows = chunk(pair, part * tokens)
            direct = skip * both_ref[:, rows, :].astype(jnp.float32)
            out_ref[:, rows, :] = (sums[:, :, part * LANES : (part + 1) * LANES] + direct).astype(bf16)
        tap_grad = sums[:, :, taps].astype(bf16)
        taps_ref[:, :, :, chunk(pair), :] = tap_grad.reshape(taps_ref.shape[:3] + (2 * SUB, LANES))

    leaving = []
    for turn in range(Y_PLACES):
        leaving.append(
            pltpu.make_async_copy(taps_ref.at[:, place_at(turn)], tap_outs[turn], out_sems.at[turn])
        )
        leaving[-1].start()
    for copy in leaving:
        copy.wait()


def join_kernel(*refs):
    parts, (kept_ref, sent_ref) = refs[:-2], refs[-2:]
    here = place()[0]
    for pair, out_ref in ((here, kept_ref), (Z_PAIRS - 1 - here, sent_ref)):
        total = parts[0][pair].astype(jnp.float32)
        for part in parts[1:]:
            total = total + part[pair].astype(jnp.float32)
        out_ref[...] = total.astype(out_ref.dtype)


def finish_kernel(kept_ref, came_ref, out_ref):
    blocks, rows, channels = kept_ref.shape
    for block in range(blocks):
        total = kept_ref[block] + came_ref[block].astype(jnp.float32)
        out_ref[:, block * rows : (block + 1) * rows] = jnp.transpose(total)


def call(kernel, args, outs, scratch, limit, flops=0, moved=0):
    in_specs = []
    held = []
    for arg, space in args:
        held.append(arg if space in (None, pl.ANY) else pltpu.with_memory_space_constraint(arg, space))
        in_specs.append(pl.BlockSpec(memory_space=pl.ANY if space in (pl.ANY, pltpu.HBM) else VMEM))
    out_shape = []
    out_specs = []
    for shape, dtype, space in outs:
        out_shape.append(jax.ShapeDtypeStruct(shape, dtype) if space is None else space(shape, dtype))
        out_specs.append(pl.BlockSpec(memory_space=pl.ANY if space is pltpu.HBM else VMEM))
    return pl.pallas_call(
        kernel,
        out_shape=tuple(out_shape),
        in_specs=in_specs,
        out_specs=tuple(out_specs),
        scratch_shapes=scratch,
        cost_estimate=pl.CostEstimate(flops=flops, bytes_accessed=moved, transcendentals=0),
        compiler_params=pltpu.CompilerParams(vmem_limit_bytes=limit * MEGA),
    )(*held)


def along_dp(array, pairs, places):
    sources = [(pair, place) for pair in range(Z_PAIRS) for place in range(Y_PLACES)]
    moves = [
        (pair * Y_PLACES + place, (pair + pairs) % Z_PAIRS * Y_PLACES + (place + places) % Y_PLACES)
        for pair, place in sources
    ]
    return lax.ppermute(array, "dp", moves)


def exchange(array, other=lambda whole: whole):
    always = lax.optimization_barrier(jnp.int32(1)) == 1
    return lax.cond(
        always,
        lambda whole: lax.all_to_all(whole, "seq", split_axis=0, concat_axis=0, tiled=True),
        other,
        array,
    )


def middle(both, taps, skip):
    groups, both_rows, channels = both.shape
    tokens = both_rows // 2
    length = groups * tokens
    ahead, back, second, undo = (jnp.asarray(table) for table in transform_tables(groups, tokens, length ** (-0.5)))
    steps = ahead.shape[0]
    far, free, dma = pltpu.HBM, None, pltpu.SemaphoreType.DMA
    tap_pair = (taps[0].shape, bf16, far)
    wide = (2 * groups, tokens, 3 * channels)
    out, *tap_grads = call(
        middle_kernel,
        [(both, pl.ANY)]
        + [(part, pl.ANY) for part in taps]
        + [
            (skip, free),
            (ahead, far),
            (back, far),
            (second, free),
            (undo, free),
        ],
        [(both.shape, bf16, VMEM)] + [tap_pair] * Y_PLACES,
        [
            VMEM(both.shape, bf16),
            VMEM((Z_PAIRS, Y_PLACES) + taps[0].shape[1:], bf16),
            VMEM(wide, bf16),
            VMEM(wide, jnp.float32),
            VMEM(ahead.shape, bf16),
            VMEM(back.shape, bf16),
            dma(()),
            dma((Y_PLACES,)),
            dma((Y_PLACES,)),
            dma((TABLE_PIECES,)),
            dma(()),
        ],
        32,
        flops=2 * 24 * length * 256 * channels,
        moved=24 * length * channels,
    )
    return out, tap_grads


def local(query, key_stream, value_stream, upstream, bases, base_rows, long_filter, skip_weight):
    groups = lax.axis_size("seq")
    tokens, width = query.shape[1:]
    length = tokens * groups
    channels = long_filter.shape[0]
    array_bytes = tokens * width * 2
    far, free, dma = pltpu.HBM, None, pltpu.SemaphoreType.DMA
    packed = ((groups, 2 * tokens, channels), bf16, VMEM)
    tap_block = (TAP_BLOCKS, tokens, channels)

    (turned,) = call(
        turn_kernel,
        [(long_filter, far)],
        [(tap_block, bf16, free)],
        [VMEM((TAP_BLOCKS, channels, tokens), jnp.float32), dma((TAP_BLOCKS,))],
        4,
    )
    other = along_dp(turned, 1, 0)
    (gates,) = call(
        gate_kernel,
        [(query, far), (key_stream, far), (value_stream, far), (upstream, far), (bases, far), (base_rows, far)],
        [packed],
        [
            VMEM((4, tokens, width), bf16),
            VMEM(bases.shape, bases.dtype),
            VMEM(base_rows.shape, bf16),
            dma((4, PIECES)),
            dma((2,)),
        ],
        12,
        moved=6 * array_bytes,
    )
    own_taps = jnp.where(place()[0] == 0, jnp.stack([turned, other]), jnp.stack([other, turned]))
    gates, own_taps = lax.optimization_barrier((gates, own_taps))
    taps = [own_taps] + [along_dp(own_taps, 0, turn) for turn in range(1, Y_PLACES)]
    both = exchange(gates)

    out, tap_grads = middle(both, taps, skip_weight.reshape(1, channels))
    came = [along_dp(tap_grads[turn], 0, turn) for turn in range(1, Y_PLACES)]
    home, *came = lax.optimization_barrier((exchange(out, lambda whole: whole + whole), *came))

    kept, sent = call(
        join_kernel,
        [(part, free) for part in [tap_grads[0]] + came],
        [(tap_block, jnp.float32, free), (tap_block, bf16, free)],
        [],
        8,
    )
    last = along_dp(sent, 1, 0)
    grad = (query.shape, bf16, far)
    query_grad, key_grad, value_grad = call(
        ungate_kernel,
        [(home, VMEM), (key_stream, far), (value_stream, far), (upstream, far), (bases, free), (base_rows, free)],
        [grad, grad, grad],
        [
            VMEM((3, tokens, width), bf16),
            dma((3, PIECES)),
            VMEM((3, tokens, width), bf16),
            dma((3, PIECES)),
        ],
        16,
        moved=6 * array_bytes,
    )
    (filter_grad,) = call(finish_kernel, [(kept, free), (last, free)], [(long_filter.shape, jnp.float32, free)], [], 8)
    return (query_grad, key_grad, value_grad, filter_grad)


def solution(mesh):
    return jax.shard_map(
        local,
        mesh=mesh,
        in_specs=(
            P("dp", "seq", None),
            P("dp", "seq", None),
            P("dp", "seq", None),
            P("dp", "seq", None),
            P("dp", "seq"),
            P(),
            P("seq", "dp"),
            P("seq"),
        ),
        out_specs=(
            P("dp", "seq", None),
            P("dp", "seq", None),
            P("dp", "seq", None),
            P("seq", "dp"),
        ),
        check_vma=False,
    )
```

```python
import math

import jax
import jax.numpy as jnp
import ml_dtypes
import numpy as np
from jax import lax
from jax.experimental import pallas as pl
from jax.experimental.pallas import tpu as pltpu
from jax.sharding import PartitionSpec as P

LANES = 128
SUB = 8
PIECES = 4
Z_PAIRS = 2
Y_PLACES = 4
TAP_BLOCKS = 4
TABLE_PIECES = 2
MEGA = 1024 * 1024
VMEM = pltpu.VMEM
bf16 = jnp.bfloat16


def transform_tables(blocks, rows, scale):
    points = 2 * blocks * rows
    low = 2 * np.arange(blocks)[:, None, None] + 1
    point = np.arange(blocks)[None, None, :] * rows + np.arange(rows)[None, :, None]
    angle = math.pi / points * (low * point % (2 * points))
    first = np.stack([np.cos(angle), -np.sin(angle)], axis=1)
    first = first.reshape(2 * blocks, rows // SUB, SUB, blocks)
    ahead = np.einsum("mhaj,ab->hmajb", first, np.eye(SUB))
    ahead = ahead.reshape(rows // SUB, 2 * blocks * SUB, blocks * SUB)
    back = np.ascontiguousarray(np.swapaxes(ahead, 1, 2))

    row = np.arange(rows)
    angle = 2.0 * math.pi / rows * (row[:, None] * row[None, :] % rows)
    cosine, sine = np.cos(angle), np.sin(angle)
    second = np.block([[cosine, sine], [-sine, cosine]])
    undo = np.ascontiguousarray(second.T) * (2.0 / points * scale)
    return tuple(table.astype(ml_dtypes.bfloat16) for table in (ahead, back, second, undo))


def dot(left, right):
    return jnp.dot(left, right, preferred_element_type=jnp.float32)


def letters_of(bases_ref):
    count = bases_ref.shape[1]
    return jnp.transpose(jnp.broadcast_to(bases_ref[...], (count, count)))


def readout(letters, rows_ref, columns):
    rows = rows_ref[:, columns].astype(jnp.float32)
    picked = rows[0:1]
    for letter in range(1, rows.shape[0]):
        picked = jnp.where(letters == letter, rows[letter : letter + 1], picked)
    return picked


def gate_kernel(query, key, value, upstream, bases, rows, out_ref, held, bases_ref, rows_ref, sems, small_sems):
    tokens, width = query.shape[1:]
    span = tokens // PIECES
    small = [
        pltpu.make_async_copy(bases, bases_ref, small_sems.at[0]),
        pltpu.make_async_copy(rows, rows_ref, small_sems.at[1]),
    ]
    copies = []
    for piece in range(PIECES):
        part = pl.ds(piece * span, span)
        copies.append([])
        for which, source in enumerate((query, key, value, upstream)):
            copies[-1].append(
                pltpu.make_async_copy(source.at[0, part], held.at[which, part], sems.at[which, piece])
            )
            copies[-1][-1].start()
        if piece == 0:
            for copy in small:
                copy.start()
    for copy in small:
        copy.wait()
    letters = letters_of(bases_ref)
    for piece in range(PIECES):
        part = slice(piece * span, (piece + 1) * span)
        here = letters[part]
        for copy in copies[piece]:
            copy.wait()
        for block in range(width // LANES):
            columns = slice(block * LANES, (block + 1) * LANES)
            query_rows, key_rows, value_rows, upstream_rows = (
                held[which, part, columns].astype(jnp.float32) for which in range(4)
            )
            out_grad = upstream_rows - readout(here, rows_ref, columns)
            out_ref[block, part, :] = (key_rows * value_rows).astype(bf16)
            out_ref[block, tokens + part.start : tokens + part.stop, :] = (out_grad * query_rows).astype(bf16)


def ungate_kernel(back_ref, key, value, upstream, bases_ref, rows_ref, *rest):
    outs, (held, in_sems, made, out_sems) = rest[:3], rest[3:]
    tokens, width = key.shape[1:]
    span = tokens // PIECES
    arriving = []
    for piece in range(PIECES):
        part = pl.ds(piece * span, span)
        arriving.append([])
        for which, source in enumerate((key, value, upstream)):
            arriving[-1].append(
                pltpu.make_async_copy(source.at[0, part], held.at[which, part], in_sems.at[which, piece])
            )
            arriving[-1][-1].start()
    letters = letters_of(bases_ref)
    leaving = []
    for piece in range(PIECES):
        part = slice(piece * span, (piece + 1) * span)
        here = letters[part]
        for copy in arriving[piece]:
            copy.wait()
        for block in range(width // LANES):
            columns = slice(block * LANES, (block + 1) * LANES)
            conv = back_ref[block, part, :].astype(jnp.float32)
            corr = back_ref[block, tokens + part.start : tokens + part.stop, :].astype(jnp.float32)
            key_rows, value_rows, upstream_rows = (held[which, part, columns].astype(jnp.float32) for which in range(3))
            out_grad = upstream_rows - readout(here, rows_ref, columns)
            made[0, part, columns] = (out_grad * conv).astype(bf16)
            made[1, part, columns] = (corr * value_rows).astype(bf16)
            made[2, part, columns] = (corr * key_rows).astype(bf16)
        part = pl.ds(piece * span, span)
        for which, target in enumerate(outs):
            copy = pltpu.make_async_copy(made.at[which, part], target.at[0, part], out_sems.at[which, piece])
            copy.start()
            leaving.append(copy)
    for copy in leaving:
        copy.wait()


def turn_kernel(taps_hbm, out_ref, held, sems):
    copies = []
    for block in range(held.shape[0]):
        columns = pl.ds(block * LANES, LANES)
        copies.append(pltpu.make_async_copy(taps_hbm.at[:, columns], held.at[block], sems.at[block]))
        copies[-1].start()
    for block, copy in enumerate(copies):
        copy.wait()
        out_ref[block] = jnp.transpose(held[block]).astype(bf16)


def chunk(pair, first=0):
    return slice(first + pair * 2 * SUB, first + (pair + 1) * 2 * SUB)


def first_stage(load, table, mid_ref):
    for pair in range(mid_ref.shape[1] // (2 * SUB)):
        both = load(pair)
        halves = []
        for part in range(2):
            piece = both[:, part * SUB : (part + 1) * SUB, :]
            piece = piece.reshape(piece.shape[0] * SUB, piece.shape[2]).astype(bf16)
            mid = dot(table(2 * pair + part), piece)
            halves.append(mid.reshape(-1, SUB, mid.shape[1]))
        mid_ref[:, chunk(pair), :] = jnp.concatenate(halves, axis=1).astype(bf16)


def last_stage(table, wide_ref, pair, columns):
    halves = []
    for step in (2 * pair, 2 * pair + 1):
        piece = wide_ref[:, step * SUB : (step + 1) * SUB, columns]
        piece = piece.reshape(piece.shape[0] * SUB, piece.shape[2]).astype(bf16)
        out = dot(table(step), piece)
        halves.append(out.reshape(-1, SUB, out.shape[1]))
    return jnp.concatenate(halves, axis=1)


def times(left, right, conjugate):
    half = left.shape[0] // 2
    left_real, left_imag = left[:half], left[half:]
    right_real, right_imag = right[:half], right[half:]
    if conjugate:
        real = left_real * right_real + left_imag * right_imag
        imag = left_imag * right_real - left_real * right_imag
    else:
        real = left_real * right_real - left_imag * right_imag
        imag = left_imag * right_real + left_real * right_imag
    return jnp.concatenate([real, imag], axis=0)


def place():
    index = lax.axis_index("dp")
    return index // Y_PLACES, lax.rem(index, Y_PLACES)


def place_at(turn):
    return lax.rem(place()[1] + turn + Y_PLACES, Y_PLACES)


def middle_kernel(both_hbm, *refs):
    taps_hbm, refs = refs[:Y_PLACES], refs[Y_PLACES:]
    (skip_ref, ahead_hbm, back_hbm, second_ref, undo_ref, out_ref), refs = refs[:6], refs[6:]
    tap_outs, refs = refs[:Y_PLACES], refs[Y_PLACES:]
    both_ref, taps_ref, mid_ref, wide_ref, ahead_ref, back_ref = refs[:6]
    both_sem, taps_sems, out_sems, ahead_sems, back_sem = refs[6:]
    groups = both_ref.shape[0]
    tokens = both_ref.shape[1] // 2
    steps = ahead_ref.shape[0]
    span = steps // TABLE_PIECES
    ahead_copies = []
    for piece in range(TABLE_PIECES):
        rows = pl.ds(piece * span, span)
        ahead_copies.append(pltpu.make_async_copy(ahead_hbm.at[rows], ahead_ref.at[rows], ahead_sems.at[piece]))
    back_copy = pltpu.make_async_copy(back_hbm, back_ref, back_sem)
    ahead_copies[0].start()
    arriving = [pltpu.make_async_copy(both_hbm, both_ref, both_sem)]
    arriving[-1].start()
    for turn in range(Y_PLACES):
        arriving.append(
            pltpu.make_async_copy(taps_hbm[turn], taps_ref.at[:, place_at(-turn)], taps_sems.at[turn])
        )
        arriving[-1].start()
    for copy in ahead_copies[1:] + [back_copy]:
        copy.start()
    for copy in arriving:
        copy.wait()

    def load(pair):
        filt = taps_ref[:, :, :, chunk(pair), :].reshape(groups, 2 * SUB, LANES)
        parts = [both_ref[:, chunk(pair), :], both_ref[:, chunk(pair, tokens), :], filt]
        return jnp.concatenate(parts, axis=2).astype(jnp.float32)

    def fresh_ahead(step):
        if step % span == 0:
            ahead_copies[step // span].wait()
        return ahead_ref[step]

    first_stage(load, fresh_ahead, mid_ref)

    def group_of(group, columns):
        both = mid_ref[2 * group : 2 * group + 2, :, columns]
        return both.reshape(2 * tokens, both.shape[2])

    second, undo = second_ref[...], undo_ref[...]
    signals, taps = slice(0, 2 * LANES), slice(2 * LANES, 3 * LANES)
    for pair in range(groups // 2):
        here = (2 * pair, 2 * pair + 1)
        filters = dot(second, jnp.concatenate([group_of(group, taps) for group in here], axis=1))
        crosses = []
        for which, group in enumerate(here):
            spectrum = dot(second, group_of(group, signals))
            gated, grad = spectrum[:, :LANES], spectrum[:, LANES:]
            filt = filters[:, which * LANES : (which + 1) * LANES]
            product = jnp.concatenate([times(gated, filt, False), times(grad, filt, True)], axis=1)
            undone = dot(undo, product.astype(bf16))
            wide_ref[2 * group : 2 * group + 2, :, signals] = undone.reshape(2, tokens, 2 * LANES)
            crosses.append(times(grad, gated, True))
        undone = dot(undo, jnp.concatenate(crosses, axis=1).astype(bf16))
        for which, group in enumerate(here):
            part = undone[:, which * LANES : (which + 1) * LANES]
            wide_ref[2 * group : 2 * group + 2, :, taps] = part.reshape(2, tokens, LANES)

    skip = skip_ref[...]

    back_copy.wait()

    for pair in range(steps // 2):
        tap_grad = last_stage(lambda step: back_ref[step], wide_ref, pair, taps).astype(bf16)
        taps_ref[:, :, :, chunk(pair), :] = tap_grad.reshape(taps_ref.shape[:3] + (2 * SUB, LANES))
    leaving = []
    for turn in range(Y_PLACES):
        leaving.append(
            pltpu.make_async_copy(taps_ref.at[:, place_at(turn)], tap_outs[turn], out_sems.at[turn])
        )
        leaving[-1].start()
    for pair in range(steps // 2):
        sums = last_stage(lambda step: back_ref[step], wide_ref, pair, signals)
        for part in range(2):
            rows = chunk(pair, part * tokens)
            direct = skip * both_ref[:, rows, :].astype(jnp.float32)
            out_ref[:, rows, :] = (sums[:, :, part * LANES : (part + 1) * LANES] + direct).astype(bf16)
    for copy in leaving:
        copy.wait()


def join_kernel(*refs):
    parts, (kept_ref, sent_ref) = refs[:-2], refs[-2:]
    here = place()[0]
    for pair, out_ref in ((here, kept_ref), (Z_PAIRS - 1 - here, sent_ref)):
        total = parts[0][pair].astype(jnp.float32)
        for part in parts[1:]:
            total = total + part[pair].astype(jnp.float32)
        out_ref[...] = total.astype(out_ref.dtype)


def finish_kernel(kept_ref, came_ref, out_ref):
    blocks, rows, channels = kept_ref.shape
    for block in range(blocks):
        total = kept_ref[block] + came_ref[block].astype(jnp.float32)
        out_ref[:, block * rows : (block + 1) * rows] = jnp.transpose(total)


def call(kernel, args, outs, scratch, limit, flops=0, moved=0):
    in_specs = []
    held = []
    for arg, space in args:
        held.append(arg if space in (None, pl.ANY) else pltpu.with_memory_space_constraint(arg, space))
        in_specs.append(pl.BlockSpec(memory_space=pl.ANY if space in (pl.ANY, pltpu.HBM) else VMEM))
    out_shape = []
    out_specs = []
    for shape, dtype, space in outs:
        out_shape.append(jax.ShapeDtypeStruct(shape, dtype) if space is None else space(shape, dtype))
        out_specs.append(pl.BlockSpec(memory_space=pl.ANY if space is pltpu.HBM else VMEM))
    return pl.pallas_call(
        kernel,
        out_shape=tuple(out_shape),
        in_specs=in_specs,
        out_specs=tuple(out_specs),
        scratch_shapes=scratch,
        cost_estimate=pl.CostEstimate(flops=flops, bytes_accessed=moved, transcendentals=0),
        compiler_params=pltpu.CompilerParams(vmem_limit_bytes=limit * MEGA),
    )(*held)


def along_dp(array, pairs, places):
    sources = [(pair, place) for pair in range(Z_PAIRS) for place in range(Y_PLACES)]
    moves = [
        (pair * Y_PLACES + place, (pair + pairs) % Z_PAIRS * Y_PLACES + (place + places) % Y_PLACES)
        for pair, place in sources
    ]
    return lax.ppermute(array, "dp", moves)


def exchange(array, other=lambda whole: whole):
    always = lax.optimization_barrier(jnp.int32(1)) == 1
    return lax.cond(
        always,
        lambda whole: lax.all_to_all(whole, "seq", split_axis=0, concat_axis=0, tiled=True),
        other,
        array,
    )


def middle(both, taps, skip):
    groups, both_rows, channels = both.shape
    tokens = both_rows // 2
    length = groups * tokens
    ahead, back, second, undo = (jnp.asarray(table) for table in transform_tables(groups, tokens, length ** (-0.5)))
    steps = ahead.shape[0]
    far, free, dma = pltpu.HBM, None, pltpu.SemaphoreType.DMA
    tap_pair = (taps[0].shape, bf16, far)
    wide = (2 * groups, tokens, 3 * channels)
    out, *tap_grads = call(
        middle_kernel,
        [(both, pl.ANY)]
        + [(part, pl.ANY) for part in taps]
        + [
            (skip, free),
            (ahead, far),
            (back, far),
            (second, free),
            (undo, free),
        ],
        [(both.shape, bf16, VMEM)] + [tap_pair] * Y_PLACES,
        [
            VMEM(both.shape, bf16),
            VMEM((Z_PAIRS, Y_PLACES) + taps[0].shape[1:], bf16),
            VMEM(wide, bf16),
            VMEM(wide, jnp.float32),
            VMEM(ahead.shape, bf16),
            VMEM(back.shape, bf16),
            dma(()),
            dma((Y_PLACES,)),
            dma((Y_PLACES,)),
            dma((TABLE_PIECES,)),
            dma(()),
        ],
        32,
        flops=2 * 24 * length * 256 * channels,
        moved=24 * length * channels,
    )
    return out, tap_grads


def gate(query, key_stream, value_stream, upstream, bases, base_rows, channels):
    tokens, width = query.shape[1:]
    far, dma = pltpu.HBM, pltpu.SemaphoreType.DMA
    (gates,) = call(
        gate_kernel,
        [(query, far), (key_stream, far), (value_stream, far), (upstream, far), (bases, far), (base_rows, far)],
        [((width // channels, 2 * tokens, channels), bf16, VMEM)],
        [
            VMEM((4, tokens, width), bf16),
            VMEM(bases.shape, bases.dtype),
            VMEM(base_rows.shape, bf16),
            dma((4, PIECES)),
            dma((2,)),
        ],
        12,
        moved=12 * tokens * width,
    )
    return gates


def ungate(home, key_stream, value_stream, upstream, bases, base_rows):
    tokens, width = key_stream.shape[1:]
    far, free, dma = pltpu.HBM, None, pltpu.SemaphoreType.DMA
    grad = (key_stream.shape, bf16, far)
    return call(
        ungate_kernel,
        [(home, VMEM), (key_stream, far), (value_stream, far), (upstream, far), (bases, free), (base_rows, free)],
        [grad, grad, grad],
        [
            VMEM((3, tokens, width), bf16),
            dma((3, PIECES)),
            VMEM((3, tokens, width), bf16),
            dma((3, PIECES)),
        ],
        16,
        moved=12 * tokens * width,
    )


def local(query, key_stream, value_stream, upstream, bases, base_rows, long_filter, skip_weight):
    groups = lax.axis_size("seq")
    tokens, width = query.shape[1:]
    length = tokens * groups
    channels = long_filter.shape[0]
    far, free, dma = pltpu.HBM, None, pltpu.SemaphoreType.DMA
    tap_block = (TAP_BLOCKS, tokens, channels)

    (turned,) = call(
        turn_kernel,
        [(long_filter, far)],
        [(tap_block, bf16, free)],
        [VMEM((TAP_BLOCKS, channels, tokens), jnp.float32), dma((TAP_BLOCKS,))],
        4,
    )
    other = along_dp(turned, 1, 0)
    gates = gate(query, key_stream, value_stream, upstream, bases, base_rows, channels)
    own_taps = jnp.where(place()[0] == 0, jnp.stack([turned, other]), jnp.stack([other, turned]))
    gates, own_taps = lax.optimization_barrier((gates, own_taps))
    taps = [own_taps] + [along_dp(own_taps, 0, turn) for turn in range(1, Y_PLACES)]
    both = exchange(gates)

    out, tap_grads = middle(both, taps, skip_weight.reshape(1, channels))
    came = [along_dp(tap_grads[turn], 0, turn) for turn in range(1, Y_PLACES)]
    home, *came = lax.optimization_barrier((exchange(out, lambda whole: whole + whole), *came))

    kept, sent = call(
        join_kernel,
        [(part, free) for part in [tap_grads[0]] + came],
        [(tap_block, jnp.float32, free), (tap_block, bf16, free)],
        [],
        8,
    )
    last = along_dp(sent, 1, 0)
    query_grad, key_grad, value_grad = ungate(home, key_stream, value_stream, upstream, bases, base_rows)
    (filter_grad,) = call(finish_kernel, [(kept, free), (last, free)], [(long_filter.shape, jnp.float32, free)], [], 8)
    return (query_grad, key_grad, value_grad, filter_grad)


def solution(mesh):
    return jax.shard_map(
        local,
        mesh=mesh,
        in_specs=(
            P("dp", "seq", None),
            P("dp", "seq", None),
            P("dp", "seq", None),
            P("dp", "seq", None),
            P("dp", "seq"),
            P(),
            P("seq", "dp"),
            P("seq"),
        ),
        out_specs=(
            P("dp", "seq", None),
            P("dp", "seq", None),
            P("dp", "seq", None),
            P("seq", "dp"),
        ),
        check_vma=False,
    )
```

```python
import math

import jax
import jax.numpy as jnp
import ml_dtypes
import numpy as np
from jax import lax
from jax.experimental import pallas as pl
from jax.experimental.pallas import tpu as pltpu
from jax.sharding import PartitionSpec as P

LANES = 128
SUB = 8
PIECES = 4
Z_PAIRS = 2
Y_PLACES = 4
TAP_BLOCKS = 4
TABLE_PIECES = 2
MEGA = 1024 * 1024
VMEM = pltpu.VMEM
bf16 = jnp.bfloat16


def transform_tables(blocks, rows, scale):
    points = 2 * blocks * rows
    low = 2 * np.arange(blocks)[:, None, None] + 1
    point = np.arange(blocks)[None, None, :] * rows + np.arange(rows)[None, :, None]
    angle = math.pi / points * (low * point % (2 * points))
    first = np.stack([np.cos(angle), -np.sin(angle)], axis=1)
    first = first.reshape(2 * blocks, rows // SUB, SUB, blocks)
    ahead = np.einsum("mhaj,ab->hmajb", first, np.eye(SUB))
    ahead = ahead.reshape(rows // SUB, 2 * blocks * SUB, blocks * SUB)
    back = np.ascontiguousarray(np.swapaxes(ahead, 1, 2))

    row = np.arange(rows)
    angle = 2.0 * math.pi / rows * (row[:, None] * row[None, :] % rows)
    cosine, sine = np.cos(angle), np.sin(angle)
    second = np.block([[cosine, sine], [-sine, cosine]])
    undo = np.ascontiguousarray(second.T) * (2.0 / points * scale)
    return tuple(table.astype(ml_dtypes.bfloat16) for table in (ahead, back, second, undo))


def dot(left, right):
    return jnp.dot(left, right, preferred_element_type=jnp.float32)


def letters_of(bases_ref):
    count = bases_ref.shape[1]
    return jnp.transpose(jnp.broadcast_to(bases_ref[...], (count, count)))


def readout(letters, rows_ref, columns):
    rows = rows_ref[:, columns].astype(jnp.float32)
    picked = rows[0:1]
    for letter in range(1, rows.shape[0]):
        picked = jnp.where(letters == letter, rows[letter : letter + 1], picked)
    return picked


def gate_kernel(query, key, value, upstream, bases, rows, out_ref, held, bases_ref, rows_ref, sems, small_sems):
    tokens, width = query.shape[1:]
    span = tokens // PIECES
    small = [
        pltpu.make_async_copy(bases, bases_ref, small_sems.at[0]),
        pltpu.make_async_copy(rows, rows_ref, small_sems.at[1]),
    ]
    copies = []
    for piece in range(PIECES):
        part = pl.ds(piece * span, span)
        copies.append([])
        for which, source in enumerate((query, key, value, upstream)):
            copies[-1].append(
                pltpu.make_async_copy(source.at[0, part], held.at[which, part], sems.at[which, piece])
            )
            copies[-1][-1].start()
        if piece == 0:
            for copy in small:
                copy.start()
    for copy in small:
        copy.wait()
    letters = letters_of(bases_ref)
    for piece in range(PIECES):
        part = slice(piece * span, (piece + 1) * span)
        here = letters[part]
        for copy in copies[piece]:
            copy.wait()
        for block in range(width // LANES):
            columns = slice(block * LANES, (block + 1) * LANES)
            query_rows, key_rows, value_rows, upstream_rows = (
                held[which, part, columns].astype(jnp.float32) for which in range(4)
            )
            out_grad = upstream_rows - readout(here, rows_ref, columns)
            out_ref[block, part, :] = (key_rows * value_rows).astype(bf16)
            out_ref[block, tokens + part.start : tokens + part.stop, :] = (out_grad * query_rows).astype(bf16)


def ungate_kernel(back_ref, key, value, upstream, bases_ref, rows_ref, *rest):
    outs, (held, in_sems, made, out_sems) = rest[:3], rest[3:]
    tokens, width = key.shape[1:]
    span = tokens // PIECES
    arriving = []
    for piece in range(PIECES):
        part = pl.ds(piece * span, span)
        arriving.append([])
        for which, source in enumerate((key, value, upstream)):
            arriving[-1].append(
                pltpu.make_async_copy(source.at[0, part], held.at[which, part], in_sems.at[which, piece])
            )
            arriving[-1][-1].start()
    letters = letters_of(bases_ref)
    leaving = []
    for piece in range(PIECES):
        part = slice(piece * span, (piece + 1) * span)
        here = letters[part]
        for copy in arriving[piece]:
            copy.wait()
        for block in range(width // LANES):
            columns = slice(block * LANES, (block + 1) * LANES)
            conv = back_ref[block, part, :].astype(jnp.float32)
            corr = back_ref[block, tokens + part.start : tokens + part.stop, :].astype(jnp.float32)
            key_rows, value_rows, upstream_rows = (held[which, part, columns].astype(jnp.float32) for which in range(3))
            out_grad = upstream_rows - readout(here, rows_ref, columns)
            made[0, part, columns] = (out_grad * conv).astype(bf16)
            made[1, part, columns] = (corr * value_rows).astype(bf16)
            made[2, part, columns] = (corr * key_rows).astype(bf16)
        part = pl.ds(piece * span, span)
        for which, target in enumerate(outs):
            copy = pltpu.make_async_copy(made.at[which, part], target.at[0, part], out_sems.at[which, piece])
            copy.start()
            leaving.append(copy)
    for copy in leaving:
        copy.wait()


def turn_kernel(taps_hbm, out_ref, held, sems):
    copies = []
    for block in range(held.shape[0]):
        columns = pl.ds(block * LANES, LANES)
        copies.append(pltpu.make_async_copy(taps_hbm.at[:, columns], held.at[block], sems.at[block]))
        copies[-1].start()
    for block, copy in enumerate(copies):
        copy.wait()
        out_ref[block] = jnp.transpose(held[block]).astype(bf16)


def chunk(pair, first=0):
    return slice(first + pair * 2 * SUB, first + (pair + 1) * 2 * SUB)


def first_stage(load, table, mid_ref):
    for pair in range(mid_ref.shape[1] // (2 * SUB)):
        both = load(pair)
        halves = []
        for part in range(2):
            piece = both[:, part * SUB : (part + 1) * SUB, :]
            piece = piece.reshape(piece.shape[0] * SUB, piece.shape[2]).astype(bf16)
            mid = dot(table(2 * pair + part), piece)
            halves.append(mid.reshape(-1, SUB, mid.shape[1]))
        mid_ref[:, chunk(pair), :] = jnp.concatenate(halves, axis=1).astype(bf16)


def last_stage(table, wide_ref, pair, columns):
    halves = []
    for step in (2 * pair, 2 * pair + 1):
        piece = wide_ref[:, step * SUB : (step + 1) * SUB, columns]
        piece = piece.reshape(piece.shape[0] * SUB, piece.shape[2]).astype(bf16)
        out = dot(table(step), piece)
        halves.append(out.reshape(-1, SUB, out.shape[1]))
    return jnp.concatenate(halves, axis=1)


def times(left, right, conjugate):
    half = left.shape[0] // 2
    left_real, left_imag = left[:half], left[half:]
    right_real, right_imag = right[:half], right[half:]
    if conjugate:
        real = left_real * right_real + left_imag * right_imag
        imag = left_imag * right_real - left_real * right_imag
    else:
        real = left_real * right_real - left_imag * right_imag
        imag = left_imag * right_real + left_real * right_imag
    return jnp.concatenate([real, imag], axis=0)


def place():
    index = lax.axis_index("dp")
    return index // Y_PLACES, lax.rem(index, Y_PLACES)


def place_at(turn):
    return lax.rem(place()[1] + turn + Y_PLACES, Y_PLACES)


def middle_kernel(both_hbm, *refs):
    taps_hbm, refs = refs[:Y_PLACES], refs[Y_PLACES:]
    (skip_ref, ahead_hbm, back_hbm, second_ref, undo_ref, out_ref), refs = refs[:6], refs[6:]
    tap_outs, refs = refs[:Y_PLACES], refs[Y_PLACES:]
    both_ref, taps_ref, mid_ref, wide_ref, ahead_ref, back_ref = refs[:6]
    both_sem, taps_sems, out_sems, ahead_sems, back_sem = refs[6:]
    groups = both_ref.shape[0]
    tokens = both_ref.shape[1] // 2
    steps = ahead_ref.shape[0]
    span = steps // TABLE_PIECES
    ahead_copies = []
    for piece in range(TABLE_PIECES):
        rows = pl.ds(piece * span, span)
        ahead_copies.append(pltpu.make_async_copy(ahead_hbm.at[rows], ahead_ref.at[rows], ahead_sems.at[piece]))
    back_copy = pltpu.make_async_copy(back_hbm, back_ref, back_sem)
    ahead_copies[0].start()
    arriving = [pltpu.make_async_copy(both_hbm, both_ref, both_sem)]
    arriving[-1].start()
    for turn in range(Y_PLACES):
        arriving.append(
            pltpu.make_async_copy(taps_hbm[turn], taps_ref.at[:, place_at(-turn)], taps_sems.at[turn])
        )
        arriving[-1].start()
    for copy in ahead_copies[1:] + [back_copy]:
        copy.start()
    for copy in arriving:
        copy.wait()

    def load(pair):
        filt = taps_ref[:, :, :, chunk(pair), :].reshape(groups, 2 * SUB, LANES)
        parts = [both_ref[:, chunk(pair), :], both_ref[:, chunk(pair, tokens), :], filt]
        return jnp.concatenate(parts, axis=2).astype(jnp.float32)

    def fresh_ahead(step):
        if step % span == 0:
            ahead_copies[step // span].wait()
        return ahead_ref[step]

    first_stage(load, fresh_ahead, mid_ref)

    def group_of(group, columns):
        both = mid_ref[2 * group : 2 * group + 2, :, columns]
        return both.reshape(2 * tokens, both.shape[2])

    second, undo = second_ref[...], undo_ref[...]
    signals, taps = slice(0, 2 * LANES), slice(2 * LANES, 3 * LANES)
    def spectra_of(pair):
        here = (2 * pair, 2 * pair + 1)
        filters = dot(second, jnp.concatenate([group_of(group, taps) for group in here], axis=1))
        return [dot(second, group_of(group, signals)) for group in here], filters

    ready = spectra_of(0)
    for pair in range(groups // 2):
        here = (2 * pair, 2 * pair + 1)
        spectra, filters = ready
        products = []
        crosses = []
        for which in range(2):
            gated, grad = spectra[which][:, :LANES], spectra[which][:, LANES:]
            filt = filters[:, which * LANES : (which + 1) * LANES]
            products.append(jnp.concatenate([times(gated, filt, False), times(grad, filt, True)], axis=1).astype(bf16))
            crosses.append(times(grad, gated, True))
        if pair + 1 < groups // 2:
            ready = spectra_of(pair + 1)
        for which, group in enumerate(here):
            undone = dot(undo, products[which])
            wide_ref[2 * group : 2 * group + 2, :, signals] = undone.reshape(2, tokens, 2 * LANES)
        undone = dot(undo, jnp.concatenate(crosses, axis=1).astype(bf16))
        for which, group in enumerate(here):
            part = undone[:, which * LANES : (which + 1) * LANES]
            wide_ref[2 * group : 2 * group + 2, :, taps] = part.reshape(2, tokens, LANES)

    skip = skip_ref[...]

    back_copy.wait()

    for pair in range(steps // 2):
        tap_grad = last_stage(lambda step: back_ref[step], wide_ref, pair, taps).astype(bf16)
        taps_ref[:, :, :, chunk(pair), :] = tap_grad.reshape(taps_ref.shape[:3] + (2 * SUB, LANES))
    leaving = []
    for turn in range(Y_PLACES):
        leaving.append(
            pltpu.make_async_copy(taps_ref.at[:, place_at(turn)], tap_outs[turn], out_sems.at[turn])
        )
        leaving[-1].start()
    for pair in range(steps // 2):
        sums = last_stage(lambda step: back_ref[step], wide_ref, pair, signals)
        for part in range(2):
            rows = chunk(pair, part * tokens)
            direct = skip * both_ref[:, rows, :].astype(jnp.float32)
            out_ref[:, rows, :] = (sums[:, :, part * LANES : (part + 1) * LANES] + direct).astype(bf16)
    for copy in leaving:
        copy.wait()


def join_kernel(*refs):
    parts, (kept_ref, sent_ref) = refs[:-2], refs[-2:]
    here = place()[0]
    for pair, out_ref in ((here, kept_ref), (Z_PAIRS - 1 - here, sent_ref)):
        total = parts[0][pair].astype(jnp.float32)
        for part in parts[1:]:
            total = total + part[pair].astype(jnp.float32)
        out_ref[...] = total.astype(out_ref.dtype)


def finish_kernel(kept_ref, came_ref, out_ref):
    blocks, rows, channels = kept_ref.shape
    for block in range(blocks):
        total = kept_ref[block] + came_ref[block].astype(jnp.float32)
        out_ref[:, block * rows : (block + 1) * rows] = jnp.transpose(total)


def call(kernel, args, outs, scratch, limit, flops=0, moved=0):
    in_specs = []
    held = []
    for arg, space in args:
        held.append(arg if space in (None, pl.ANY) else pltpu.with_memory_space_constraint(arg, space))
        in_specs.append(pl.BlockSpec(memory_space=pl.ANY if space in (pl.ANY, pltpu.HBM) else VMEM))
    out_shape = []
    out_specs = []
    for shape, dtype, space in outs:
        out_shape.append(jax.ShapeDtypeStruct(shape, dtype) if space is None else space(shape, dtype))
        out_specs.append(pl.BlockSpec(memory_space=pl.ANY if space is pltpu.HBM else VMEM))
    return pl.pallas_call(
        kernel,
        out_shape=tuple(out_shape),
        in_specs=in_specs,
        out_specs=tuple(out_specs),
        scratch_shapes=scratch,
        cost_estimate=pl.CostEstimate(flops=flops, bytes_accessed=moved, transcendentals=0),
        compiler_params=pltpu.CompilerParams(vmem_limit_bytes=limit * MEGA),
    )(*held)


def along_dp(array, pairs, places):
    sources = [(pair, place) for pair in range(Z_PAIRS) for place in range(Y_PLACES)]
    moves = [
        (pair * Y_PLACES + place, (pair + pairs) % Z_PAIRS * Y_PLACES + (place + places) % Y_PLACES)
        for pair, place in sources
    ]
    return lax.ppermute(array, "dp", moves)


def exchange(array, other=lambda whole: whole):
    always = lax.optimization_barrier(jnp.int32(1)) == 1
    return lax.cond(
        always,
        lambda whole: lax.all_to_all(whole, "seq", split_axis=0, concat_axis=0, tiled=True),
        other,
        array,
    )


def middle(both, taps, skip):
    groups, both_rows, channels = both.shape
    tokens = both_rows // 2
    length = groups * tokens
    ahead, back, second, undo = (jnp.asarray(table) for table in transform_tables(groups, tokens, length ** (-0.5)))
    steps = ahead.shape[0]
    far, free, dma = pltpu.HBM, None, pltpu.SemaphoreType.DMA
    tap_pair = (taps[0].shape, bf16, far)
    wide = (2 * groups, tokens, 3 * channels)
    out, *tap_grads = call(
        middle_kernel,
        [(both, pl.ANY)]
        + [(part, pl.ANY) for part in taps]
        + [
            (skip, free),
            (ahead, far),
            (back, far),
            (second, free),
            (undo, free),
        ],
        [(both.shape, bf16, VMEM)] + [tap_pair] * Y_PLACES,
        [
            VMEM(both.shape, bf16),
            VMEM((Z_PAIRS, Y_PLACES) + taps[0].shape[1:], bf16),
            VMEM(wide, bf16),
            VMEM(wide, jnp.float32),
            VMEM(ahead.shape, bf16),
            VMEM(back.shape, bf16),
            dma(()),
            dma((Y_PLACES,)),
            dma((Y_PLACES,)),
            dma((TABLE_PIECES,)),
            dma(()),
        ],
        32,
        flops=2 * 24 * length * 256 * channels,
        moved=24 * length * channels,
    )
    return out, tap_grads


def gate(query, key_stream, value_stream, upstream, bases, base_rows, channels):
    tokens, width = query.shape[1:]
    far, dma = pltpu.HBM, pltpu.SemaphoreType.DMA
    (gates,) = call(
        gate_kernel,
        [(query, far), (key_stream, far), (value_stream, far), (upstream, far), (bases, far), (base_rows, far)],
        [((width // channels, 2 * tokens, channels), bf16, VMEM)],
        [
            VMEM((4, tokens, width), bf16),
            VMEM(bases.shape, bases.dtype),
            VMEM(base_rows.shape, bf16),
            dma((4, PIECES)),
            dma((2,)),
        ],
        12,
        moved=12 * tokens * width,
    )
    return gates


def ungate(home, key_stream, value_stream, upstream, bases, base_rows):
    tokens, width = key_stream.shape[1:]
    far, free, dma = pltpu.HBM, None, pltpu.SemaphoreType.DMA
    grad = (key_stream.shape, bf16, far)
    return call(
        ungate_kernel,
        [(home, VMEM), (key_stream, far), (value_stream, far), (upstream, far), (bases, free), (base_rows, free)],
        [grad, grad, grad],
        [
            VMEM((3, tokens, width), bf16),
            dma((3, PIECES)),
            VMEM((3, tokens, width), bf16),
            dma((3, PIECES)),
        ],
        16,
        moved=12 * tokens * width,
    )


def local(query, key_stream, value_stream, upstream, bases, base_rows, long_filter, skip_weight):
    groups = lax.axis_size("seq")
    tokens, width = query.shape[1:]
    length = tokens * groups
    channels = long_filter.shape[0]
    far, free, dma = pltpu.HBM, None, pltpu.SemaphoreType.DMA
    tap_block = (TAP_BLOCKS, tokens, channels)

    (turned,) = call(
        turn_kernel,
        [(long_filter, far)],
        [(tap_block, bf16, free)],
        [VMEM((TAP_BLOCKS, channels, tokens), jnp.float32), dma((TAP_BLOCKS,))],
        4,
    )
    other = along_dp(turned, 1, 0)
    gates = gate(query, key_stream, value_stream, upstream, bases, base_rows, channels)
    own_taps = jnp.where(place()[0] == 0, jnp.stack([turned, other]), jnp.stack([other, turned]))
    gates, own_taps = lax.optimization_barrier((gates, own_taps))
    taps = [own_taps] + [along_dp(own_taps, 0, turn) for turn in range(1, Y_PLACES)]
    both = exchange(gates)

    out, tap_grads = middle(both, taps, skip_weight.reshape(1, channels))
    came = [along_dp(tap_grads[turn], 0, turn) for turn in range(1, Y_PLACES)]
    home, *came = lax.optimization_barrier((exchange(out, lambda whole: whole + whole), *came))

    kept, sent = call(
        join_kernel,
        [(part, free) for part in [tap_grads[0]] + came],
        [(tap_block, jnp.float32, free), (tap_block, bf16, free)],
        [],
        8,
    )
    last = along_dp(sent, 1, 0)
    query_grad, key_grad, value_grad = ungate(home, key_stream, value_stream, upstream, bases, base_rows)
    (filter_grad,) = call(finish_kernel, [(kept, free), (last, free)], [(long_filter.shape, jnp.float32, free)], [], 8)
    return (query_grad, key_grad, value_grad, filter_grad)


def solution(mesh):
    return jax.shard_map(
        local,
        mesh=mesh,
        in_specs=(
            P("dp", "seq", None),
            P("dp", "seq", None),
            P("dp", "seq", None),
            P("dp", "seq", None),
            P("dp", "seq"),
            P(),
            P("seq", "dp"),
            P("seq"),
        ),
        out_specs=(
            P("dp", "seq", None),
            P("dp", "seq", None),
            P("dp", "seq", None),
            P("seq", "dp"),
        ),
        check_vma=False,
    )
```

```python
import math

import jax
import jax.numpy as jnp
import ml_dtypes
import numpy as np
from jax import lax
from jax.experimental import pallas as pl
from jax.experimental.pallas import tpu as pltpu
from jax.sharding import PartitionSpec as P

LANES = 128
SUB = 8
GATE_PIECES = 2
PIECES = 4
Z_PAIRS = 2
Y_PLACES = 4
TAP_BLOCKS = 4
TABLE_PIECES = 2
MEGA = 1024 * 1024
VMEM = pltpu.VMEM
bf16 = jnp.bfloat16


def transform_tables(blocks, rows, scale):
    points = 2 * blocks * rows
    low = 2 * np.arange(blocks)[:, None, None] + 1
    point = np.arange(blocks)[None, None, :] * rows + np.arange(rows)[None, :, None]
    angle = math.pi / points * (low * point % (2 * points))
    first = np.stack([np.cos(angle), -np.sin(angle)], axis=1)
    first = first.reshape(2 * blocks, rows // SUB, SUB, blocks)
    ahead = np.einsum("mhaj,ab->hmajb", first, np.eye(SUB))
    ahead = ahead.reshape(rows // SUB, 2 * blocks * SUB, blocks * SUB)
    back = np.ascontiguousarray(np.swapaxes(ahead, 1, 2))

    row = np.arange(rows)
    angle = 2.0 * math.pi / rows * (row[:, None] * row[None, :] % rows)
    cosine, sine = np.cos(angle), np.sin(angle)
    second = np.block([[cosine, sine], [-sine, cosine]])
    undo = np.ascontiguousarray(second.T) * (2.0 / points * scale)
    return tuple(table.astype(ml_dtypes.bfloat16) for table in (ahead, back, second, undo))


def dot(left, right):
    return jnp.dot(left, right, preferred_element_type=jnp.float32)


def letters_of(bases_ref):
    count = bases_ref.shape[1]
    return jnp.transpose(jnp.broadcast_to(bases_ref[...], (count, count)))


def readout(letters, rows_ref, columns):
    rows = rows_ref[:, columns].astype(jnp.float32)
    picked = rows[0:1]
    for letter in range(1, rows.shape[0]):
        picked = jnp.where(letters == letter, rows[letter : letter + 1], picked)
    return picked


def gate_kernel(query, key, value, upstream, bases, rows, out_ref, held, bases_ref, rows_ref, sems, small_sems):
    tokens, width = query.shape[1:]
    span = tokens // GATE_PIECES
    small = [
        pltpu.make_async_copy(bases, bases_ref, small_sems.at[0]),
        pltpu.make_async_copy(rows, rows_ref, small_sems.at[1]),
    ]
    copies = []
    for piece in range(GATE_PIECES):
        part = pl.ds(piece * span, span)
        copies.append([])
        for which, source in enumerate((query, key, value, upstream)):
            copies[-1].append(
                pltpu.make_async_copy(source.at[0, part], held.at[which, part], sems.at[which, piece])
            )
            copies[-1][-1].start()
        if piece == 0:
            for copy in small:
                copy.start()
    for copy in small:
        copy.wait()
    letters = letters_of(bases_ref)
    for piece in range(GATE_PIECES):
        part = slice(piece * span, (piece + 1) * span)
        here = letters[part]
        for copy in copies[piece]:
            copy.wait()
        for block in range(width // LANES):
            columns = slice(block * LANES, (block + 1) * LANES)
            query_rows, key_rows, value_rows, upstream_rows = (
                held[which, part, columns].astype(jnp.float32) for which in range(4)
            )
            out_grad = upstream_rows - readout(here, rows_ref, columns)
            out_ref[block, part, :] = (key_rows * value_rows).astype(bf16)
            out_ref[block, tokens + part.start : tokens + part.stop, :] = (out_grad * query_rows).astype(bf16)


def ungate_kernel(back_ref, key, value, upstream, bases_ref, rows_ref, *rest):
    outs, (held, in_sems, made, out_sems) = rest[:3], rest[3:]
    tokens, width = key.shape[1:]
    span = tokens // PIECES
    arriving = []
    for piece in range(PIECES):
        part = pl.ds(piece * span, span)
        arriving.append([])
        for which, source in enumerate((key, value, upstream)):
            arriving[-1].append(
                pltpu.make_async_copy(source.at[0, part], held.at[which, part], in_sems.at[which, piece])
            )
            arriving[-1][-1].start()
    letters = letters_of(bases_ref)
    leaving = []
    for piece in range(PIECES):
        part = slice(piece * span, (piece + 1) * span)
        here = letters[part]
        for copy in arriving[piece]:
            copy.wait()
        for block in range(width // LANES):
            columns = slice(block * LANES, (block + 1) * LANES)
            conv = back_ref[block, part, :].astype(jnp.float32)
            corr = back_ref[block, tokens + part.start : tokens + part.stop, :].astype(jnp.float32)
            key_rows, value_rows, upstream_rows = (held[which, part, columns].astype(jnp.float32) for which in range(3))
            out_grad = upstream_rows - readout(here, rows_ref, columns)
            made[0, part, columns] = (out_grad * conv).astype(bf16)
            made[1, part, columns] = (corr * value_rows).astype(bf16)
            made[2, part, columns] = (corr * key_rows).astype(bf16)
        part = pl.ds(piece * span, span)
        for which, target in enumerate(outs):
            copy = pltpu.make_async_copy(made.at[which, part], target.at[0, part], out_sems.at[which, piece])
            copy.start()
            leaving.append(copy)
    for copy in leaving:
        copy.wait()


def turn_kernel(taps_hbm, out_ref, held, sem):
    copy = pltpu.make_async_copy(taps_hbm, held, sem)
    copy.start()
    copy.wait()
    for block in range(out_ref.shape[0]):
        out_ref[block] = jnp.transpose(held[:, block * LANES : (block + 1) * LANES]).astype(bf16)


def chunk(pair, first=0):
    return slice(first + pair * 2 * SUB, first + (pair + 1) * 2 * SUB)


def first_stage(load, table, mid_ref):
    for pair in range(mid_ref.shape[1] // (2 * SUB)):
        both = load(pair)
        halves = []
        for part in range(2):
            piece = both[:, part * SUB : (part + 1) * SUB, :]
            piece = piece.reshape(piece.shape[0] * SUB, piece.shape[2]).astype(bf16)
            mid = dot(table(2 * pair + part), piece)
            halves.append(mid.reshape(-1, SUB, mid.shape[1]))
        mid_ref[:, chunk(pair), :] = jnp.concatenate(halves, axis=1).astype(bf16)


def last_stage(table, wide_ref, pair, columns):
    halves = []
    for step in (2 * pair, 2 * pair + 1):
        piece = wide_ref[:, step * SUB : (step + 1) * SUB, columns]
        piece = piece.reshape(piece.shape[0] * SUB, piece.shape[2]).astype(bf16)
        out = dot(table(step), piece)
        halves.append(out.reshape(-1, SUB, out.shape[1]))
    return jnp.concatenate(halves, axis=1)


def times(left, right, conjugate):
    half = left.shape[0] // 2
    left_real, left_imag = left[:half], left[half:]
    right_real, right_imag = right[:half], right[half:]
    if conjugate:
        real = left_real * right_real + left_imag * right_imag
        imag = left_imag * right_real - left_real * right_imag
    else:
        real = left_real * right_real - left_imag * right_imag
        imag = left_imag * right_real + left_real * right_imag
    return jnp.concatenate([real, imag], axis=0)


def place():
    index = lax.axis_index("dp")
    return index // Y_PLACES, lax.rem(index, Y_PLACES)


def place_at(turn):
    return lax.rem(place()[1] + turn + Y_PLACES, Y_PLACES)


def middle_kernel(both_hbm, *refs):
    taps_hbm, refs = refs[:Y_PLACES], refs[Y_PLACES:]
    (skip_ref, ahead_hbm, back_hbm, second_ref, undo_ref, out_ref), refs = refs[:6], refs[6:]
    tap_outs, refs = refs[:Y_PLACES], refs[Y_PLACES:]
    both_ref, taps_ref, mid_ref, wide_ref, ahead_ref, back_ref = refs[:6]
    both_sem, taps_sems, out_sems, ahead_sems, back_sem = refs[6:]
    groups = both_ref.shape[0]
    tokens = both_ref.shape[1] // 2
    steps = ahead_ref.shape[0]
    span = steps // TABLE_PIECES
    ahead_copies = []
    for piece in range(TABLE_PIECES):
        rows = pl.ds(piece * span, span)
        ahead_copies.append(pltpu.make_async_copy(ahead_hbm.at[rows], ahead_ref.at[rows], ahead_sems.at[piece]))
    back_copy = pltpu.make_async_copy(back_hbm, back_ref, back_sem)
    ahead_copies[0].start()
    arriving = [pltpu.make_async_copy(both_hbm, both_ref, both_sem)]
    arriving[-1].start()
    for turn in range(Y_PLACES):
        arriving.append(
            pltpu.make_async_copy(taps_hbm[turn], taps_ref.at[:, place_at(-turn)], taps_sems.at[turn])
        )
        arriving[-1].start()
    for copy in ahead_copies[1:] + [back_copy]:
        copy.start()
    for copy in arriving:
        copy.wait()

    def load(pair):
        filt = taps_ref[:, :, :, chunk(pair), :].reshape(groups, 2 * SUB, LANES)
        parts = [both_ref[:, chunk(pair), :], both_ref[:, chunk(pair, tokens), :], filt]
        return jnp.concatenate(parts, axis=2).astype(jnp.float32)

    def fresh_ahead(step):
        if step % span == 0:
            ahead_copies[step // span].wait()
        return ahead_ref[step]

    first_stage(load, fresh_ahead, mid_ref)

    def group_of(group, columns):
        both = mid_ref[2 * group : 2 * group + 2, :, columns]
        return both.reshape(2 * tokens, both.shape[2])

    second, undo = second_ref[...], undo_ref[...]
    signals, taps = slice(0, 2 * LANES), slice(2 * LANES, 3 * LANES)
    def spectra_of(pair):
        here = (2 * pair, 2 * pair + 1)
        filters = dot(second, jnp.concatenate([group_of(group, taps) for group in here], axis=1))
        return [dot(second, group_of(group, signals)) for group in here], filters

    ready = spectra_of(0)
    for pair in range(groups // 2):
        here = (2 * pair, 2 * pair + 1)
        spectra, filters = ready
        products = []
        crosses = []
        for which in range(2):
            gated, grad = spectra[which][:, :LANES], spectra[which][:, LANES:]
            filt = filters[:, which * LANES : (which + 1) * LANES]
            products.append(jnp.concatenate([times(gated, filt, False), times(grad, filt, True)], axis=1).astype(bf16))
            crosses.append(times(grad, gated, True))
        if pair + 1 < groups // 2:
            ready = spectra_of(pair + 1)
        for which, group in enumerate(here):
            undone = dot(undo, products[which])
            wide_ref[2 * group : 2 * group + 2, :, signals] = undone.reshape(2, tokens, 2 * LANES)
        undone = dot(undo, jnp.concatenate(crosses, axis=1).astype(bf16))
        for which, group in enumerate(here):
            part = undone[:, which * LANES : (which + 1) * LANES]
            wide_ref[2 * group : 2 * group + 2, :, taps] = part.reshape(2, tokens, LANES)

    skip = skip_ref[...]

    back_copy.wait()

    for pair in range(steps // 2):
        tap_grad = last_stage(lambda step: back_ref[step], wide_ref, pair, taps).astype(bf16)
        taps_ref[:, :, :, chunk(pair), :] = tap_grad.reshape(taps_ref.shape[:3] + (2 * SUB, LANES))
    leaving = []
    for turn in range(Y_PLACES):
        leaving.append(
            pltpu.make_async_copy(taps_ref.at[:, place_at(turn)], tap_outs[turn], out_sems.at[turn])
        )
        leaving[-1].start()
    for pair in range(steps // 2):
        sums = last_stage(lambda step: back_ref[step], wide_ref, pair, signals)
        for part in range(2):
            rows = chunk(pair, part * tokens)
            direct = skip * both_ref[:, rows, :].astype(jnp.float32)
            out_ref[:, rows, :] = (sums[:, :, part * LANES : (part + 1) * LANES] + direct).astype(bf16)
    for copy in leaving:
        copy.wait()


def join_kernel(*refs):
    parts, (kept_ref, sent_ref) = refs[:-2], refs[-2:]
    here = place()[0]
    for pair, out_ref in ((here, kept_ref), (Z_PAIRS - 1 - here, sent_ref)):
        total = parts[0][pair].astype(jnp.float32)
        for part in parts[1:]:
            total = total + part[pair].astype(jnp.float32)
        out_ref[...] = total.astype(out_ref.dtype)


def finish_kernel(kept_ref, came_ref, out_ref):
    blocks, rows, channels = kept_ref.shape
    for block in range(blocks):
        total = kept_ref[block] + came_ref[block].astype(jnp.float32)
        out_ref[:, block * rows : (block + 1) * rows] = jnp.transpose(total)


def call(kernel, args, outs, scratch, limit, flops=0, moved=0):
    in_specs = []
    held = []
    for arg, space in args:
        held.append(arg if space in (None, pl.ANY) else pltpu.with_memory_space_constraint(arg, space))
        in_specs.append(pl.BlockSpec(memory_space=pl.ANY if space in (pl.ANY, pltpu.HBM) else VMEM))
    out_shape = []
    out_specs = []
    for shape, dtype, space in outs:
        out_shape.append(jax.ShapeDtypeStruct(shape, dtype) if space is None else space(shape, dtype))
        out_specs.append(pl.BlockSpec(memory_space=pl.ANY if space is pltpu.HBM else VMEM))
    return pl.pallas_call(
        kernel,
        out_shape=tuple(out_shape),
        in_specs=in_specs,
        out_specs=tuple(out_specs),
        scratch_shapes=scratch,
        cost_estimate=pl.CostEstimate(flops=flops, bytes_accessed=moved, transcendentals=0),
        compiler_params=pltpu.CompilerParams(vmem_limit_bytes=limit * MEGA),
    )(*held)


def along_dp(array, pairs, places):
    sources = [(pair, place) for pair in range(Z_PAIRS) for place in range(Y_PLACES)]
    moves = [
        (pair * Y_PLACES + place, (pair + pairs) % Z_PAIRS * Y_PLACES + (place + places) % Y_PLACES)
        for pair, place in sources
    ]
    return lax.ppermute(array, "dp", moves)


def exchange(array, other=lambda whole: whole):
    always = lax.optimization_barrier(jnp.int32(1)) == 1
    return lax.cond(
        always,
        lambda whole: lax.all_to_all(whole, "seq", split_axis=0, concat_axis=0, tiled=True),
        other,
        array,
    )


def middle(both, taps, skip):
    groups, both_rows, channels = both.shape
    tokens = both_rows // 2
    length = groups * tokens
    ahead, back, second, undo = (jnp.asarray(table) for table in transform_tables(groups, tokens, length ** (-0.5)))
    steps = ahead.shape[0]
    far, free, dma = pltpu.HBM, None, pltpu.SemaphoreType.DMA
    tap_pair = (taps[0].shape, bf16, far)
    wide = (2 * groups, tokens, 3 * channels)
    out, *tap_grads = call(
        middle_kernel,
        [(both, pl.ANY)]
        + [(part, pl.ANY) for part in taps]
        + [
            (skip, free),
            (ahead, far),
            (back, far),
            (second, free),
            (undo, free),
        ],
        [(both.shape, bf16, VMEM)] + [tap_pair] * Y_PLACES,
        [
            VMEM(both.shape, bf16),
            VMEM((Z_PAIRS, Y_PLACES) + taps[0].shape[1:], bf16),
            VMEM(wide, bf16),
            VMEM(wide, jnp.float32),
            VMEM(ahead.shape, bf16),
            VMEM(back.shape, bf16),
            dma(()),
            dma((Y_PLACES,)),
            dma((Y_PLACES,)),
            dma((TABLE_PIECES,)),
            dma(()),
        ],
        32,
        flops=2 * 24 * length * 256 * channels,
        moved=24 * length * channels,
    )
    return out, tap_grads


def gate(query, key_stream, value_stream, upstream, bases, base_rows, channels):
    tokens, width = query.shape[1:]
    far, dma = pltpu.HBM, pltpu.SemaphoreType.DMA
    (gates,) = call(
        gate_kernel,
        [(query, far), (key_stream, far), (value_stream, far), (upstream, far), (bases, far), (base_rows, far)],
        [((width // channels, 2 * tokens, channels), bf16, VMEM)],
        [
            VMEM((4, tokens, width), bf16),
            VMEM(bases.shape, bases.dtype),
            VMEM(base_rows.shape, bf16),
            dma((4, GATE_PIECES)),
            dma((2,)),
        ],
        12,
        moved=12 * tokens * width,
    )
    return gates


def ungate(home, key_stream, value_stream, upstream, bases, base_rows):
    tokens, width = key_stream.shape[1:]
    far, free, dma = pltpu.HBM, None, pltpu.SemaphoreType.DMA
    grad = (key_stream.shape, bf16, far)
    return call(
        ungate_kernel,
        [(home, VMEM), (key_stream, far), (value_stream, far), (upstream, far), (bases, free), (base_rows, free)],
        [grad, grad, grad],
        [
            VMEM((3, tokens, width), bf16),
            dma((3, PIECES)),
            VMEM((3, tokens, width), bf16),
            dma((3, PIECES)),
        ],
        16,
        moved=12 * tokens * width,
    )


def local(query, key_stream, value_stream, upstream, bases, base_rows, long_filter, skip_weight):
    groups = lax.axis_size("seq")
    tokens, width = query.shape[1:]
    length = tokens * groups
    channels = long_filter.shape[0]
    far, free, dma = pltpu.HBM, None, pltpu.SemaphoreType.DMA
    tap_block = (TAP_BLOCKS, tokens, channels)

    (turned,) = call(
        turn_kernel,
        [(long_filter, far)],
        [(tap_block, bf16, free)],
        [VMEM(long_filter.shape, jnp.float32), dma(())],
        4,
    )
    other = along_dp(turned, 1, 0)
    gates = gate(query, key_stream, value_stream, upstream, bases, base_rows, channels)
    own_taps = jnp.where(place()[0] == 0, jnp.stack([turned, other]), jnp.stack([other, turned]))
    gates, own_taps = lax.optimization_barrier((gates, own_taps))
    taps = [own_taps] + [along_dp(own_taps, 0, turn) for turn in range(1, Y_PLACES)]
    both = exchange(gates)

    out, tap_grads = middle(both, taps, skip_weight.reshape(1, channels))
    came = [along_dp(tap_grads[turn], 0, turn) for turn in range(1, Y_PLACES)]
    home, *came = lax.optimization_barrier((exchange(out, lambda whole: whole + whole), *came))

    kept, sent = call(
        join_kernel,
        [(part, free) for part in [tap_grads[0]] + came],
        [(tap_block, jnp.float32, free), (tap_block, bf16, free)],
        [],
        8,
    )
    last = along_dp(sent, 1, 0)
    query_grad, key_grad, value_grad = ungate(home, key_stream, value_stream, upstream, bases, base_rows)
    (filter_grad,) = call(finish_kernel, [(kept, free), (last, free)], [(long_filter.shape, jnp.float32, free)], [], 8)
    return (query_grad, key_grad, value_grad, filter_grad)


def solution(mesh):
    return jax.shard_map(
        local,
        mesh=mesh,
        in_specs=(
            P("dp", "seq", None),
            P("dp", "seq", None),
            P("dp", "seq", None),
            P("dp", "seq", None),
            P("dp", "seq"),
            P(),
            P("seq", "dp"),
            P("seq"),
        ),
        out_specs=(
            P("dp", "seq", None),
            P("dp", "seq", None),
            P("dp", "seq", None),
            P("seq", "dp"),
        ),
        check_vma=False,
    )
```

```python
import math

import jax
import jax.numpy as jnp
import ml_dtypes
import numpy as np
from jax import lax
from jax.experimental import pallas as pl
from jax.experimental.pallas import tpu as pltpu
from jax.sharding import PartitionSpec as P

LANES = 128
SUB = 8
GATE_PIECES = 2
PIECES = 4
Z_PAIRS = 2
Y_PLACES = 4
TAP_BLOCKS = 4
TABLE_PIECES = 2
MEGA = 1024 * 1024
VMEM = pltpu.VMEM
bf16 = jnp.bfloat16


def transform_tables(blocks, rows, scale):
    points = 2 * blocks * rows
    low = 2 * np.arange(blocks)[:, None, None] + 1
    point = np.arange(blocks)[None, None, :] * rows + np.arange(rows)[None, :, None]
    angle = math.pi / points * (low * point % (2 * points))
    first = np.stack([np.cos(angle), -np.sin(angle)], axis=1)
    first = first.reshape(2 * blocks, rows // SUB, SUB, blocks)
    ahead = np.einsum("mhaj,ab->hmajb", first, np.eye(SUB))
    ahead = ahead.reshape(rows // SUB, 2 * blocks * SUB, blocks * SUB)
    back = np.ascontiguousarray(np.swapaxes(ahead, 1, 2))

    row = np.arange(rows)
    angle = 2.0 * math.pi / rows * (row[:, None] * row[None, :] % rows)
    cosine, sine = np.cos(angle), np.sin(angle)
    second = np.block([[cosine, sine], [-sine, cosine]])
    undo = np.ascontiguousarray(second.T) * (2.0 / points * scale)
    return tuple(table.astype(ml_dtypes.bfloat16) for table in (ahead, back, second, undo))


def dot(left, right):
    return jnp.dot(left, right, preferred_element_type=jnp.float32)


def letters_of(bases_ref):
    count = bases_ref.shape[1]
    return jnp.transpose(jnp.broadcast_to(bases_ref[...], (count, count)))


def readout(letters, rows_ref, columns):
    rows = rows_ref[:, columns].astype(jnp.float32)
    picked = rows[0:1]
    for letter in range(1, rows.shape[0]):
        picked = jnp.where(letters == letter, rows[letter : letter + 1], picked)
    return picked


def gate_kernel(query, key, value, upstream, bases, rows, out_ref, held, bases_ref, rows_ref, sems, small_sems):
    tokens, width = query.shape[1:]
    span = tokens // GATE_PIECES
    small = [
        pltpu.make_async_copy(bases, bases_ref, small_sems.at[0]),
        pltpu.make_async_copy(rows, rows_ref, small_sems.at[1]),
    ]
    copies = []
    for piece in range(GATE_PIECES):
        part = pl.ds(piece * span, span)
        copies.append([])
        for which, source in enumerate((query, key, value, upstream)):
            copies[-1].append(
                pltpu.make_async_copy(source.at[0, part], held.at[which, part], sems.at[which, piece])
            )
            copies[-1][-1].start()
        if piece == 0:
            for copy in small:
                copy.start()
    for copy in small:
        copy.wait()
    letters = letters_of(bases_ref)
    for piece in range(GATE_PIECES):
        part = slice(piece * span, (piece + 1) * span)
        here = letters[part]
        for copy in copies[piece]:
            copy.wait()
        for block in range(width // LANES):
            columns = slice(block * LANES, (block + 1) * LANES)
            query_rows, key_rows, value_rows, upstream_rows = (
                held[which, part, columns].astype(jnp.float32) for which in range(4)
            )
            out_grad = upstream_rows - readout(here, rows_ref, columns)
            out_ref[block, part, :] = (key_rows * value_rows).astype(bf16)
            out_ref[block, tokens + part.start : tokens + part.stop, :] = (out_grad * query_rows).astype(bf16)


def ungate_kernel(back_ref, key, value, upstream, bases_ref, rows_ref, *rest):
    outs, (held, in_sems, made, out_sems) = rest[:3], rest[3:]
    tokens, width = key.shape[1:]
    span = tokens // PIECES
    arriving = []
    for piece in range(PIECES):
        part = pl.ds(piece * span, span)
        arriving.append([])
        for which, source in enumerate((key, value, upstream)):
            arriving[-1].append(
                pltpu.make_async_copy(source.at[0, part], held.at[which, part], in_sems.at[which, piece])
            )
            arriving[-1][-1].start()
    letters = letters_of(bases_ref)
    leaving = []
    for piece in range(PIECES):
        part = slice(piece * span, (piece + 1) * span)
        here = letters[part]
        for copy in arriving[piece]:
            copy.wait()
        for block in range(width // LANES):
            columns = slice(block * LANES, (block + 1) * LANES)
            conv = back_ref[block, part, :].astype(jnp.float32)
            corr = back_ref[block, tokens + part.start : tokens + part.stop, :].astype(jnp.float32)
            key_rows, value_rows, upstream_rows = (held[which, part, columns].astype(jnp.float32) for which in range(3))
            out_grad = upstream_rows - readout(here, rows_ref, columns)
            made[0, part, columns] = (out_grad * conv).astype(bf16)
            made[1, part, columns] = (corr * value_rows).astype(bf16)
            made[2, part, columns] = (corr * key_rows).astype(bf16)
        part = pl.ds(piece * span, span)
        for which, target in enumerate(outs):
            copy = pltpu.make_async_copy(made.at[which, part], target.at[0, part], out_sems.at[which, piece])
            copy.start()
            leaving.append(copy)
    for copy in leaving:
        copy.wait()


def turn_kernel(taps_hbm, out_ref, held, sem):
    copy = pltpu.make_async_copy(taps_hbm, held, sem)
    copy.start()
    copy.wait()
    for block in range(out_ref.shape[0]):
        out_ref[block] = jnp.transpose(held[:, block * LANES : (block + 1) * LANES]).astype(bf16)


def chunk(pair, first=0):
    return slice(first + pair * 2 * SUB, first + (pair + 1) * 2 * SUB)


def first_stage(load, table, mid_ref):
    for pair in range(mid_ref.shape[1] // (2 * SUB)):
        both = load(pair)
        halves = []
        for part in range(2):
            piece = both[:, part * SUB : (part + 1) * SUB, :]
            piece = piece.reshape(piece.shape[0] * SUB, piece.shape[2]).astype(bf16)
            mid = dot(table(2 * pair + part), piece)
            halves.append(mid.reshape(-1, SUB, mid.shape[1]))
        mid_ref[:, chunk(pair), :] = jnp.concatenate(halves, axis=1).astype(bf16)


def last_stage(table, wide_ref, pair, columns):
    halves = []
    for step in (2 * pair, 2 * pair + 1):
        piece = wide_ref[:, step * SUB : (step + 1) * SUB, columns]
        piece = piece.reshape(piece.shape[0] * SUB, piece.shape[2]).astype(bf16)
        out = dot(table(step), piece)
        halves.append(out.reshape(-1, SUB, out.shape[1]))
    return jnp.concatenate(halves, axis=1)


def times(left, right, conjugate):
    half = left.shape[0] // 2
    left_real, left_imag = left[:half], left[half:]
    right_real, right_imag = right[:half], right[half:]
    if conjugate:
        real = left_real * right_real + left_imag * right_imag
        imag = left_imag * right_real - left_real * right_imag
    else:
        real = left_real * right_real - left_imag * right_imag
        imag = left_imag * right_real + left_real * right_imag
    return jnp.concatenate([real, imag], axis=0)


def place():
    index = lax.axis_index("dp")
    return index // Y_PLACES, lax.rem(index, Y_PLACES)


def place_at(turn):
    return lax.rem(place()[1] + turn + Y_PLACES, Y_PLACES)


def middle_kernel(both_hbm, *refs):
    taps_hbm, refs = refs[:Y_PLACES], refs[Y_PLACES:]
    (skip_ref, ahead_hbm, back_hbm, second_ref, undo_ref, out_ref), refs = refs[:6], refs[6:]
    tap_outs, refs = refs[:Y_PLACES], refs[Y_PLACES:]
    both_ref, taps_ref, mid_ref, wide_ref, ahead_ref, back_ref = refs[:6]
    both_sem, taps_sems, out_sems, ahead_sems, back_sem = refs[6:]
    groups = both_ref.shape[0]
    tokens = both_ref.shape[1] // 2
    steps = ahead_ref.shape[0]
    span = steps // TABLE_PIECES
    ahead_copies = []
    for piece in range(TABLE_PIECES):
        rows = pl.ds(piece * span, span)
        ahead_copies.append(pltpu.make_async_copy(ahead_hbm.at[rows], ahead_ref.at[rows], ahead_sems.at[piece]))
    back_copy = pltpu.make_async_copy(back_hbm, back_ref, back_sem)
    ahead_copies[0].start()
    arriving = [pltpu.make_async_copy(both_hbm, both_ref, both_sem)]
    arriving[-1].start()
    for turn in range(Y_PLACES):
        arriving.append(
            pltpu.make_async_copy(taps_hbm[turn], taps_ref.at[:, place_at(-turn)], taps_sems.at[turn])
        )
        arriving[-1].start()
    for copy in ahead_copies[1:] + [back_copy]:
        copy.start()
    for copy in arriving:
        copy.wait()

    def load(pair):
        filt = taps_ref[:, :, :, chunk(pair), :].reshape(groups, 2 * SUB, LANES)
        parts = [both_ref[:, chunk(pair), :], both_ref[:, chunk(pair, tokens), :], filt]
        return jnp.concatenate(parts, axis=2).astype(jnp.float32)

    def fresh_ahead(step):
        if step % span == 0:
            ahead_copies[step // span].wait()
        return ahead_ref[step]

    first_stage(load, fresh_ahead, mid_ref)

    def group_of(group, columns):
        both = mid_ref[2 * group : 2 * group + 2, :, columns]
        return both.reshape(2 * tokens, both.shape[2])

    second, undo = second_ref[...], undo_ref[...]
    signals, taps = slice(0, 2 * LANES), slice(2 * LANES, 3 * LANES)
    def spectra_of(pair):
        here = (2 * pair, 2 * pair + 1)
        filters = dot(second, jnp.concatenate([group_of(group, taps) for group in here], axis=1))
        return [dot(second, group_of(group, signals)) for group in here], filters

    ready = spectra_of(0)
    for pair in range(groups // 2):
        here = (2 * pair, 2 * pair + 1)
        spectra, filters = ready
        products = []
        crosses = []
        for which in range(2):
            gated, grad = spectra[which][:, :LANES], spectra[which][:, LANES:]
            filt = filters[:, which * LANES : (which + 1) * LANES]
            products.append(jnp.concatenate([times(gated, filt, False), times(grad, filt, True)], axis=1).astype(bf16))
            crosses.append(times(grad, gated, True))
        if pair + 1 < groups // 2:
            ready = spectra_of(pair + 1)
        for which, group in enumerate(here):
            undone = dot(undo, products[which])
            wide_ref[2 * group : 2 * group + 2, :, signals] = undone.reshape(2, tokens, 2 * LANES)
        undone = dot(undo, jnp.concatenate(crosses, axis=1).astype(bf16))
        for which, group in enumerate(here):
            part = undone[:, which * LANES : (which + 1) * LANES]
            wide_ref[2 * group : 2 * group + 2, :, taps] = part.reshape(2, tokens, LANES)

    skip = skip_ref[...]

    back_copy.wait()

    for pair in range(steps // 2):
        tap_grad = last_stage(lambda step: back_ref[step], wide_ref, pair, taps).astype(bf16)
        taps_ref[:, :, :, chunk(pair), :] = tap_grad.reshape(taps_ref.shape[:3] + (2 * SUB, LANES))
    leaving = []
    for turn in range(Y_PLACES):
        leaving.append(
            pltpu.make_async_copy(taps_ref.at[:, place_at(turn)], tap_outs[turn], out_sems.at[turn])
        )
        leaving[-1].start()
    for pair in range(steps // 2):
        sums = last_stage(lambda step: back_ref[step], wide_ref, pair, signals)
        for part in range(2):
            rows = chunk(pair, part * tokens)
            direct = skip * both_ref[:, rows, :].astype(jnp.float32)
            out_ref[:, rows, :] = (sums[:, :, part * LANES : (part + 1) * LANES] + direct).astype(bf16)
    for copy in leaving:
        copy.wait()


def join_kernel(*refs):
    parts, (kept_ref, sent_ref) = refs[:-2], refs[-2:]
    here = place()[0]
    for pair, out_ref in ((here, kept_ref), (Z_PAIRS - 1 - here, sent_ref)):
        total = parts[0][pair].astype(jnp.float32)
        for part in parts[1:]:
            total = total + part[pair].astype(jnp.float32)
        out_ref[...] = total.astype(out_ref.dtype)


def finish_kernel(kept_ref, came_ref, out_ref):
    blocks, rows, channels = kept_ref.shape
    for block in range(blocks):
        total = kept_ref[block] + came_ref[block].astype(jnp.float32)
        out_ref[:, block * rows : (block + 1) * rows] = jnp.transpose(total)


def call(kernel, args, outs, scratch, limit, flops=0, moved=0):
    in_specs = []
    held = []
    for arg, space in args:
        held.append(arg if space in (None, pl.ANY) else pltpu.with_memory_space_constraint(arg, space))
        in_specs.append(pl.BlockSpec(memory_space=pl.ANY if space in (pl.ANY, pltpu.HBM) else VMEM))
    out_shape = []
    out_specs = []
    for shape, dtype, space in outs:
        out_shape.append(jax.ShapeDtypeStruct(shape, dtype) if space is None else space(shape, dtype))
        out_specs.append(pl.BlockSpec(memory_space=pl.ANY if space is pltpu.HBM else VMEM))
    return pl.pallas_call(
        kernel,
        out_shape=tuple(out_shape),
        in_specs=in_specs,
        out_specs=tuple(out_specs),
        scratch_shapes=scratch,
        cost_estimate=pl.CostEstimate(flops=flops, bytes_accessed=moved, transcendentals=0),
        compiler_params=pltpu.CompilerParams(vmem_limit_bytes=limit * MEGA),
    )(*held)


def along_dp(array, pairs, places):
    sources = [(pair, place) for pair in range(Z_PAIRS) for place in range(Y_PLACES)]
    moves = [
        (pair * Y_PLACES + place, (pair + pairs) % Z_PAIRS * Y_PLACES + (place + places) % Y_PLACES)
        for pair, place in sources
    ]
    return lax.ppermute(array, "dp", moves)


def exchange(array, other=lambda whole: whole):
    always = lax.optimization_barrier(jnp.int32(1)) == 1
    return lax.cond(
        always,
        lambda whole: lax.all_to_all(whole, "seq", split_axis=0, concat_axis=0, tiled=True),
        other,
        array,
    )


def middle(both, taps, skip):
    groups, both_rows, channels = both.shape
    tokens = both_rows // 2
    length = groups * tokens
    ahead, back, second, undo = (jnp.asarray(table) for table in transform_tables(groups, tokens, length ** (-0.5)))
    steps = ahead.shape[0]
    far, free, dma = pltpu.HBM, None, pltpu.SemaphoreType.DMA
    tap_pair = (taps[0].shape, bf16, far)
    wide = (2 * groups, tokens, 3 * channels)
    out, *tap_grads = call(
        middle_kernel,
        [(both, pl.ANY)]
        + [(part, pl.ANY) for part in taps]
        + [
            (skip, free),
            (ahead, far),
            (back, far),
            (second, free),
            (undo, free),
        ],
        [(both.shape, bf16, VMEM)] + [tap_pair] * Y_PLACES,
        [
            VMEM(both.shape, bf16),
            VMEM((Z_PAIRS, Y_PLACES) + taps[0].shape[1:], bf16),
            VMEM(wide, bf16),
            VMEM(wide, jnp.float32),
            VMEM(ahead.shape, bf16),
            VMEM(back.shape, bf16),
            dma(()),
            dma((Y_PLACES,)),
            dma((Y_PLACES,)),
            dma((TABLE_PIECES,)),
            dma(()),
        ],
        32,
        flops=2 * 24 * length * 256 * channels,
        moved=24 * length * channels,
    )
    return out, tap_grads


def gate(query, key_stream, value_stream, upstream, bases, base_rows, channels):
    tokens, width = query.shape[1:]
    far, dma = pltpu.HBM, pltpu.SemaphoreType.DMA
    (gates,) = call(
        gate_kernel,
        [(query, far), (key_stream, far), (value_stream, far), (upstream, far), (bases, far), (base_rows, far)],
        [((width // channels, 2 * tokens, channels), bf16, VMEM)],
        [
            VMEM((4, tokens, width), bf16),
            VMEM(bases.shape, bases.dtype),
            VMEM(base_rows.shape, bf16),
            dma((4, GATE_PIECES)),
            dma((2,)),
        ],
        12,
        moved=12 * tokens * width,
    )
    return gates


def ungate(home, key_stream, value_stream, upstream, bases, base_rows):
    tokens, width = key_stream.shape[1:]
    far, free, dma = pltpu.HBM, None, pltpu.SemaphoreType.DMA
    grad = (key_stream.shape, bf16, far)
    return call(
        ungate_kernel,
        [(home, VMEM), (key_stream, far), (value_stream, far), (upstream, far), (bases, free), (base_rows, free)],
        [grad, grad, grad],
        [
            VMEM((3, tokens, width), bf16),
            dma((3, PIECES)),
            VMEM((3, tokens, width), bf16),
            dma((3, PIECES)),
        ],
        16,
        moved=12 * tokens * width,
    )


def local(query, key_stream, value_stream, upstream, bases, base_rows, long_filter, skip_weight):
    groups = lax.axis_size("seq")
    tokens, width = query.shape[1:]
    length = tokens * groups
    channels = long_filter.shape[0]
    far, free, dma = pltpu.HBM, None, pltpu.SemaphoreType.DMA
    tap_block = (TAP_BLOCKS, tokens, channels)

    (turned,) = call(
        turn_kernel,
        [(long_filter, far)],
        [(tap_block, bf16, free)],
        [VMEM(long_filter.shape, jnp.float32), dma(())],
        4,
    )
    other = along_dp(turned, 1, 0)
    gates = gate(query, key_stream, value_stream, upstream, bases, base_rows, channels)
    own_taps = jnp.where(place()[0] == 0, jnp.stack([turned, other]), jnp.stack([other, turned]))
    gates, own_taps = lax.optimization_barrier((gates, own_taps))
    taps = [own_taps] + [along_dp(own_taps, 0, turn) for turn in range(1, Y_PLACES)]
    both = exchange(gates)

    out, tap_grads = middle(both, taps, skip_weight.reshape(1, channels))
    came = [along_dp(tap_grads[turn], 0, turn) for turn in (2, 1, 3)]
    home, *came = lax.optimization_barrier((exchange(out, lambda whole: whole + whole), *came))

    kept, sent = call(
        join_kernel,
        [(part, free) for part in [tap_grads[0]] + came],
        [(tap_block, jnp.float32, free), (tap_block, bf16, free)],
        [],
        8,
    )
    last = along_dp(sent, 1, 0)
    query_grad, key_grad, value_grad = ungate(home, key_stream, value_stream, upstream, bases, base_rows)
    (filter_grad,) = call(finish_kernel, [(kept, free), (last, free)], [(long_filter.shape, jnp.float32, free)], [], 8)
    return (query_grad, key_grad, value_grad, filter_grad)


def solution(mesh):
    return jax.shard_map(
        local,
        mesh=mesh,
        in_specs=(
            P("dp", "seq", None),
            P("dp", "seq", None),
            P("dp", "seq", None),
            P("dp", "seq", None),
            P("dp", "seq"),
            P(),
            P("seq", "dp"),
            P("seq"),
        ),
        out_specs=(
            P("dp", "seq", None),
            P("dp", "seq", None),
            P("dp", "seq", None),
            P("seq", "dp"),
        ),
        check_vma=False,
    )
```
